128 devices in a mesh: pp: 8 (over z, x_hi), ep: 16 (over y, x_lo, core).
Axes of the slice: x: 4 (x_hi: 2, x_lo: 2; x = x_hi * 2 + x_lo), y: 4, z: 4, core: 2. Of those that a mesh axis runs over, the one named last changes fastest.
Arguments:
- fwd_in: bfloat16 [8, 1024, 3584], P('pp', 'ep'), may hold values from -100 to 100
- fwd_routes: int32 [8, 2, 1024, 2], P('pp', None, 'ep'), may hold values from 0 to 15, all different within a row; in each aligned block of 64 rows (0 to 63, 64 to 127, ..., all dimensions but the last counted through in order) at most 12 rows name the same one
- fwd_gates: float32 [8, 2, 1024, 2], P('pp', None, 'ep'), may hold values from 0.2 to 1.5
- bwd_grad: bfloat16 [8, 1024, 3584], P('pp', 'ep'), may hold values from -6 to 6
- bwd_saved: bfloat16 [8, 2, 1024, 3584], P('pp', None, 'ep'), may hold values from -100 to 100
- bwd_routes: int32 [8, 2, 1024, 2], P('pp', None, 'ep'), may hold values from 0 to 15, all different within a row; in each aligned block of 64 rows (0 to 63, 64 to 127, ..., all dimensions but the last counted through in order) at most 12 rows name the same one
- bwd_gates: float32 [8, 2, 1024, 2], P('pp', None, 'ep'), may hold values from 0.2 to 1.5
- norm_gain: float32 [8, 3584], P('pp'), may hold values from 0.1 to 1.9
- gate_w: bfloat16 [8, 16, 3584, 1024], P('pp', 'ep'), may hold values from -0.09375 to 0.09375
- up_w: bfloat16 [8, 16, 3584, 1024], P('pp', 'ep'), may hold values from -0.09375 to 0.09375
- down_w: bfloat16 [8, 16, 1024, 3584], P('pp', 'ep'), may hold values from -0.1875 to 0.1875
Outputs:
- fwd_out: bfloat16 [8, 2, 1024, 3584], P('pp', None, 'ep')
- bwd_out: bfloat16 [8, 2, 1024, 3584], P('pp', None, 'ep')
The draws below stay inside these ranges and needn't reach their ends.
Inputs may be any that keep to these rules, and one draw needn't show every extreme that they name: `fwd_routes`: A row's 2 experts differ. In each aligned block of 64 rows (one device's rows for one section and tick) no expert is named by more than 12 rows, a bound that some block reaches. `bwd_routes`: A row's 2 experts differ. In each aligned block of 64 rows (one device's rows for one section and tick) no expert is named by more than 12 rows, a bound that some block reaches.
All inputs are finite; a program needn't handle non-finite values.
Results may differ from the reference program's by a relative error of at most 0.0079.
Values may be sent and summed in bfloat16 or wider, within the bound.
A program may use at most 128 MiB of HBM per device.

```python
import math
import jax
import jax.numpy as jnp
import numpy as np
from jax import lax

D = 3584
FH = 1024
TOPW = 2
TICKS = 2
TOK_DEV = 64
EXPERTS = 16
TOKENS = 1024
CAP = 12
N_PP = 8
N_EP = 16


def textured(key, leading, spread):
    keys = jax.random.split(key, 4)
    full = leading + (D,)
    normal_part = jax.random.normal(keys[0], full, jnp.float32)
    noise = normal_part
    row_scale = jnp.exp(jax.random.uniform(keys[2], leading + (1,), jnp.float32, -spread, spread))
    col_scale = jnp.exp(jax.random.uniform(keys[3], (D,), jnp.float32, -spread, spread))
    values = noise * col_scale * row_scale
    return jnp.clip(values, -100.0, 100.0)


def draw_fwd_in(key, part):
    key = jax.random.fold_in(key, 11)
    values = textured(key, (N_PP, TOKENS), 1.15)
    return values.astype(jnp.bfloat16)


def draw_bwd_saved(key, part):
    key = jax.random.fold_in(key, 23)
    values = textured(key, (N_PP, TICKS, TOKENS), 1.15)
    return values.astype(jnp.bfloat16)


def level_of(stream_key, dims, cuts, low, high):
    def one(position, parts):
        steps = jax.random.uniform(jax.random.fold_in(jax.random.fold_in(stream_key, 6), position), (parts,), jnp.float32, low / len(cuts), high / len(cuts))
        return jnp.repeat(jnp.exp(steps), dims[position] // parts).reshape((-1,) + (1,) * (len(dims) - position - 1))

    gain = one(*cuts[0])
    for cut in cuts[1:]:
        gain = gain * one(*cut)
    return gain


def deal_out(key, own, number, rows, number_of, top, most, skew):
    order = jax.random.permutation(key, number_of)
    packed, usual = load_shares(number_of, rows * top, most, skew, True), load_shares(number_of, rows * top, most, skew, False)
    places = jnp.arange(number_of)

    def named(lengths, turn):
        used = int((lengths > 0).sum())
        fixed = max(1, used // 4)
        passed = fixed + (places - fixed + turn * (used - fixed)) % max(1, number_of - fixed)
        return jnp.zeros((number_of,), jnp.int32).at[order[jnp.where(places < fixed, places, passed)]].set(jnp.asarray(lengths, jnp.int32))

    lengths = jnp.where(number % 4 == 0, named(packed, number // 4), named(usual, number - number // 4 - 1))
    mixed = jax.random.permutation(jax.random.fold_in(own, 3), number_of)
    donor, sink = mixed[0:number_of // 2 * 2:2], mixed[1:number_of // 2 * 2:2]
    slack = jnp.minimum(lengths[donor] - 1, most - lengths[sink]) // 2
    slack = jnp.where((donor == order[0]) | (sink == order[0]) | (lengths[sink] == 0), 0, jnp.maximum(slack, 0))
    passed = jax.random.randint(jax.random.fold_in(own, 4), (number_of // 2,), 0, 1 << 20) % (slack + 1)
    lengths = lengths.at[donor].add(-passed).at[sink].add(passed)
    items = jnp.searchsorted(jnp.cumsum(lengths), jnp.arange(rows * top), side="right").astype(jnp.int32)
    listing = items.reshape(top, rows).T
    listing = listing[jax.random.permutation(jax.random.fold_in(own, 1), rows)]
    turn = jax.random.randint(jax.random.fold_in(own, 2), (rows, 1), 0, top)
    return jnp.take_along_axis(listing, (jnp.arange(top)[None, :] + turn) % top, axis=1)


def load_shares(number_of, total, reach, skew, full):
    portions = [(1 << 20) // math.isqrt(rank ** skew) + 1 for rank in range(1, number_of + 1)]
    largest = reach if full else min(reach, max(-(-total // number_of), total * portions[0] // sum(portions)))
    least = 1 if total - largest >= number_of - 1 else 0
    given, surplus = [largest] + [least] * (number_of - 1), total - largest - least * (number_of - 1)
    while surplus > 0:
        candidates = [i for i in range(1, number_of) if given[i] < largest] or [i for i in range(1, number_of) if given[i] < reach]
        whole, budget = sum([portions[i] for i in candidates]), surplus
        for i in candidates:
            addition = min(reach - given[i], max(1, budget * portions[i] // whole), surplus)
            given[i] = given[i] + addition
            surplus = surplus - addition
    return np.array(given)


def scatter_about(rng, shape, width, most, cuts=(), kind=jnp.bfloat16):
    values = width * jax.random.normal(rng, shape, jnp.float32)
    if cuts:
        values = values * level_of(rng, shape, cuts, -0.22, 0.18)
    return jnp.clip(values, -most, most).astype(kind)


def setup_inputs(seed: int = 0) -> dict:
    splits = jax.random.split(jax.random.key(seed), 12)
    fwd_in = draw_fwd_in(jax.random.fold_in(splits[11], 71), 0)
    fwd_routes_keys = jax.random.split(jax.random.fold_in(splits[1], 1), N_PP * TICKS * TOKENS // TOK_DEV)
    fwd_routes_turns = jax.random.permutation(jax.random.fold_in(splits[1], 3), N_PP * TICKS * TOKENS // TOK_DEV)
    fwd_routes = jax.vmap(lambda own, number: deal_out(jax.random.fold_in(splits[1], 2), own, number, TOK_DEV, EXPERTS, TOPW, CAP, 1))(fwd_routes_keys, fwd_routes_turns).reshape((N_PP, TICKS, TOKENS, TOPW))
    fwd_gates = jnp.clip(0.2 + 1.3 * jax.random.uniform(splits[2], (N_PP, TICKS, TOKENS, TOPW), jnp.float32) ** level_of(splits[2], (N_PP, TICKS, TOKENS, TOPW), ((0, 8), (2, 16)), -0.2, 0.2), 0.2, 1.5)
    bwd_grad = scatter_about(splits[3], (N_PP, TOKENS, D), 1.0, 6.0, ((0, 8), (1, 16)))
    bwd_saved = draw_bwd_saved(jax.random.fold_in(splits[11], 71), 0)
    bwd_routes_keys = jax.random.split(jax.random.fold_in(splits[5], 1), N_PP * TICKS * TOKENS // TOK_DEV)
    bwd_routes_turns = jax.random.permutation(jax.random.fold_in(splits[5], 3), N_PP * TICKS * TOKENS // TOK_DEV)
    bwd_routes = jax.vmap(lambda own, number: deal_out(jax.random.fold_in(splits[5], 2), own, number, TOK_DEV, EXPERTS, TOPW, CAP, 1))(bwd_routes_keys, bwd_routes_turns).reshape((N_PP, TICKS, TOKENS, TOPW))
    bwd_gates = jnp.clip(0.2 + 1.3 * jax.random.uniform(splits[6], (N_PP, TICKS, TOKENS, TOPW), jnp.float32) ** level_of(splits[6], (N_PP, TICKS, TOKENS, TOPW), ((0, 8), (2, 16)), -0.2, 0.2), 0.2, 1.5)
    norm_gain = jnp.clip(1.0 + 0.18 * jax.random.normal(splits[7], (N_PP, D), jnp.float32), 0.1, 1.9)
    gate_w = scatter_about(splits[8], (N_PP, EXPERTS, D, FH), D ** -0.5, 0.09375, ((0, 8), (1, 16)))
    up_w = scatter_about(splits[9], (N_PP, EXPERTS, D, FH), D ** -0.5, 0.09375, ((0, 8), (1, 16)))
    down_w = scatter_about(splits[10], (N_PP, EXPERTS, FH, D), FH ** -0.5, 0.1875, ((0, 8), (1, 16)))
    return dict(fwd_in=fwd_in, fwd_routes=fwd_routes, fwd_gates=fwd_gates, bwd_grad=bwd_grad, bwd_saved=bwd_saved, bwd_routes=bwd_routes, bwd_gates=bwd_gates, norm_gain=norm_gain, gate_w=gate_w, up_w=up_w, down_w=down_w)


def normed(values, norm_gain):
    scale = lax.rsqrt(lax.optimization_barrier(jnp.mean(values * values, -1, keepdims=True)) + 1e-06)
    return values * scale * norm_gain

def expert_forward(inputs, gate_mat, up_mat, down_mat):
    gate_pre = jnp.dot(inputs, gate_mat, preferred_element_type=jnp.float32)
    up_pre = jnp.dot(inputs, up_mat, preferred_element_type=jnp.float32)
    gated = (gate_pre * jax.nn.sigmoid(gate_pre) * up_pre).astype(jnp.bfloat16)
    return jnp.dot(gated, down_mat, preferred_element_type=jnp.float32).astype(jnp.bfloat16)

def expert_backward(inputs, grads, gate_mat, up_mat, down_mat):
    gate_pre = jnp.dot(inputs, gate_mat, preferred_element_type=jnp.float32)
    up_pre = jnp.dot(inputs, up_mat, preferred_element_type=jnp.float32)
    sigmoid_gate = jax.nn.sigmoid(gate_pre)
    hidden_grad = lax.dot_general(grads, down_mat, (((1,), (1,)), ((), ())), preferred_element_type=jnp.float32)
    gate_grad = (hidden_grad * up_pre * sigmoid_gate * (1.0 + gate_pre * (1.0 - sigmoid_gate))).astype(jnp.bfloat16)
    up_grad = (hidden_grad * gate_pre * sigmoid_gate).astype(jnp.bfloat16)
    result = lax.dot_general(gate_grad, gate_mat, (((1,), (1,)), ((), ())), preferred_element_type=jnp.float32)
    result = result + lax.dot_general(up_grad, up_mat, (((1,), (1,)), ((), ())), preferred_element_type=jnp.float32)
    return result.astype(jnp.bfloat16)

def by_expert(routes):
    flat_routes = routes.reshape(-1).astype(jnp.int32)
    sorted_ids = jnp.argsort(flat_routes, stable=True).astype(jnp.int32)
    expert_ids = jnp.arange(EXPERTS, dtype=jnp.int32)
    counts = lax.optimization_barrier(jnp.sum((flat_routes[:, None] == expert_ids[None, :]).astype(jnp.int32), 0))
    starts = jnp.cumsum(counts) - counts
    slot_ids = jnp.arange(N_EP * CAP, dtype=jnp.int32)
    assigned = flat_routes.shape[0]
    positions = jnp.minimum(starts[:, None] + slot_ids[None, :], assigned - 1).astype(jnp.int32)
    picked = sorted_ids[positions]
    in_use = slot_ids[None, :] < counts[:, None]
    targets = jnp.where(in_use, picked, assigned).reshape(-1).astype(jnp.int32)
    return (picked, targets)

def forward_section(acts, routes, mix_weights, norm_gain, gate_all, up_all, down_all):
    normed_rows = normed(acts.astype(jnp.float32), norm_gain).astype(jnp.bfloat16)
    picked, targets = by_expert(routes)
    token_rows = picked // TOPW

    def per_expert(pieces):
        gate_mat, up_mat, down_mat, chosen = pieces
        return expert_forward(normed_rows[chosen], gate_mat, up_mat, down_mat)
    results = lax.map(per_expert, (gate_all, up_all, down_all, token_rows))
    per_assign = jnp.zeros((TOKENS * TOPW, D), jnp.bfloat16).at[targets].set(results.reshape(-1, D), mode='drop')
    per_assign = per_assign.reshape(TOKENS, TOPW, D).astype(jnp.float32)
    mixed = acts.astype(jnp.float32) + lax.optimization_barrier(jnp.sum(mix_weights[:, :, None] * per_assign, 1))
    return mixed.astype(jnp.bfloat16)

def backward_section(cot, saved, routes, mix_weights, norm_gain, gate_all, up_all, down_all):
    saved_float = saved.astype(jnp.float32)
    normed_rows = normed(saved_float, norm_gain).astype(jnp.bfloat16)
    scaled = (mix_weights[:, :, None] * cot.astype(jnp.float32)[:, None, :]).astype(jnp.bfloat16).reshape(-1, D)
    picked, targets = by_expert(routes)
    token_rows = picked // TOPW

    def per_expert(pieces):
        gate_mat, up_mat, down_mat, chosen, rows_of = pieces
        return expert_backward(normed_rows[rows_of], scaled[chosen], gate_mat, up_mat, down_mat)
    results = lax.map(per_expert, (gate_all, up_all, down_all, picked, token_rows))
    per_assign = jnp.zeros((TOKENS * TOPW, D), jnp.bfloat16).at[targets].set(results.reshape(-1, D), mode='drop')
    summed = lax.optimization_barrier(jnp.sum(per_assign.reshape(TOKENS, TOPW, D).astype(jnp.float32), 1))
    _, pullback = jax.vjp(lambda values: normed(values, norm_gain), saved_float)
    return (cot.astype(jnp.float32) + pullback(summed)[0]).astype(jnp.bfloat16)

def reference(fwd_in, fwd_routes, fwd_gates, bwd_grad, bwd_saved, bwd_routes, bwd_gates, norm_gain, gate_w, up_w, down_w):
    carried = [fwd_in[section] for section in range(N_PP)]
    fwd_ticks = []
    for tick in range(TICKS):
        results = [forward_section(carried[section], fwd_routes[section, tick], fwd_gates[section, tick], norm_gain[section], gate_w[section], up_w[section], down_w[section]) for section in range(N_PP)]
        fwd_ticks.append(jnp.stack(results))
        carried = [jnp.zeros_like(results[0])] + results[:-1]
    carried = [bwd_grad[section] for section in range(N_PP)]
    bwd_ticks = []
    for tick in range(TICKS):
        results = [backward_section(carried[section], bwd_saved[section, tick], bwd_routes[section, tick], bwd_gates[section, tick], norm_gain[section], gate_w[section], up_w[section], down_w[section]) for section in range(N_PP)]
        bwd_ticks.append(jnp.stack(results))
        carried = results[1:] + [jnp.zeros_like(results[0])]
    return (jnp.stack(fwd_ticks, 1), jnp.stack(bwd_ticks, 1))
```

```python
import jax
import jax.numpy as jnp
from jax import lax
from jax.experimental import pallas as pl
from jax.experimental.pallas import tpu as pltpu
from jax.sharding import PartitionSpec as P

MESH = pl.DeviceIdType.MESH
BF = jnp.bfloat16
F32 = jnp.float32

EP = 16
PP = 8
TOK = 64
CAP = 12
D = 3584
FH = 1024
ROWS = EP * CAP
BLK = 16
GRP = D // 4
WIDE = 3 * GRP
PACK = EP * BLK

F0D, B0S, B0C, F0R, B1S, B0R, F1D, B1C, F1R, B1R = range(10)


def dot(a, b):
    return jnp.dot(a, b, preferred_element_type=F32)


def dot_nt(a, b):
    return lax.dot_general(a, b, (((1,), (1,)), ((), ())), preferred_element_type=F32)


def iota(shape, dim):
    return lax.broadcasted_iota(jnp.int32, shape, dim)


def one_hot(cond):
    return jnp.where(cond, 1.0, 0.0).astype(BF)


def group(q):
    return pl.ds(pl.multiple_of(q * GRP, 128), GRP)


TAIL = pl.ds(WIDE, GRP)


def kernel(
    fwd_in,
    fwd_routes,
    fwd_gates,
    bwd_grad,
    bwd_saved,
    bwd_routes,
    bwd_gates,
    gain,
    gate_hbm,
    up_hbm,
    down_hbm,
    fwd_out,
    bwd_out,
    gate_w,
    up_w,
    down_w,
    fd_s,
    fd_r,
    fr_s,
    fr_r,
    bs_s,
    bs_r,
    bc_s,
    bc_r,
    br_s,
    br_r,
    mats,
    mats_t,
    unpk,
    pck,
    tok2,
    xs,
    cs,
    h1,
    h2,
    acts1,
    cot1,
    w_sem,
    s_sem,
    r_sem,
    rel_s,
    rel_r,
):
    pp = lax.axis_index("pp")
    me = lax.axis_index("ep")
    ahead = lax.rem(pp + 1, PP)
    behind = lax.rem(pp + PP - 1, PP)

    loads = [
        pltpu.make_async_copy(src, dst, w_sem.at[i])
        for i, (src, dst) in enumerate(
            ((gate_hbm, gate_w), (up_hbm, up_w), (down_hbm, down_w))
        )
    ]
    for load in loads:
        load.start()

    barrier = pltpu.get_barrier_semaphore()

    def greet(d, carry):
        pl.semaphore_signal(
            barrier, inc=1, device_id=(pp, lax.rem(me + d, EP)), device_id_type=MESH
        )
        return carry

    lax.fori_loop(1, EP, greet, 0)
    pl.semaphore_signal(barrier, inc=1, device_id=(ahead, me), device_id_type=MESH)
    pl.semaphore_signal(barrier, inc=1, device_id=(behind, me), device_id_type=MESH)

    def block(e):
        return pl.ds(pl.multiple_of(e * BLK, BLK), BLK)

    def exchange(src, dst, phase):
        pltpu.make_async_copy(
            src.at[block(me)], dst.at[block(me)], r_sem.at[phase]
        ).start()

        def one(d, carry):
            e = lax.rem(me + d, EP)
            pltpu.make_async_remote_copy(
                src_ref=src.at[block(e)],
                dst_ref=dst.at[block(me)],
                send_sem=s_sem.at[phase],
                recv_sem=r_sem.at[phase],
                device_id=(pp, e),
                device_id_type=MESH,
            ).start()
            return carry

        lax.fori_loop(1, EP, one, 0)

    def arrived(dst, phase):
        pltpu.make_async_copy(dst, dst, r_sem.at[phase]).wait()

    def left(src, phase):
        part = src.at[pl.ds(0, PACK - BLK)]
        pltpu.make_async_copy(part, part, s_sem.at[phase]).wait()

    def relay(src, dst, which, to):
        return pltpu.make_async_remote_copy(
            src_ref=src,
            dst_ref=dst,
            send_sem=rel_s.at[which],
            recv_sem=rel_r.at[which],
            device_id=(to, me),
            device_id_type=MESH,
        )

    def slots(routes, tick, p):
        both = routes[tick]
        expert = jnp.concatenate([both[:, 0:1], both[:, 1:2]], axis=0)
        lanes = iota((2 * TOK, 128), 1)
        chosen = one_hot(expert == lanes)
        lower = one_hot(iota((2 * TOK, 2 * TOK), 1) < iota((2 * TOK, 2 * TOK), 0))
        before = dot(lower, chosen)
        slot = jnp.sum(before * chosen.astype(F32), axis=1, keepdims=True).astype(
            jnp.int32
        )
        third = (
            jnp.where(slot >= 3, 1, 0)
            + jnp.where(slot >= 6, 1, 0)
            + jnp.where(slot >= 9, 1, 0)
        )
        rest = slot - 3 * third
        cols = iota((2 * TOK, PACK), 1)
        main = jnp.where(cols == expert * BLK + slot, 1.0, 0.0)
        for q in range(3):
            tail = jnp.where(
                cols == jnp.where(rest == q, expert * BLK + CAP + third, -1), 1.0, 0.0
            )
            full = jnp.concatenate([main, tail], axis=0)
            mats[p, q] = full.astype(BF)
            mats_t[p, q] = full.T.astype(BF)

    rows = iota((ROWS, PACK), 0)
    cols = iota((ROWS, PACK), 1)
    source, slot = rows // CAP, rows % CAP
    for q in range(3):
        main = jnp.where(cols == source * BLK + slot, 1.0, 0.0)
        tail = jnp.where(
            (cols == source * BLK + CAP + slot // 3) & (slot % 3 == q), 1.0, 0.0
        )
        unpk[q, pl.ds(0, ROWS), :] = main.astype(BF)
        unpk[q, pl.ds(ROWS, ROWS), :] = tail.astype(BF)
    rows = iota((PACK, ROWS), 0)
    cols = iota((PACK, ROWS), 1)
    source, slot = cols // CAP, cols % CAP
    for q in range(3):
        main = jnp.where(rows == source * BLK + slot, 1.0, 0.0)
        tail = jnp.where(
            (rows == source * BLK + CAP + slot // 3) & (slot % 3 == q), 1.0, 0.0
        )
        pck[q] = jnp.concatenate([main, tail], axis=1).astype(BF)

    def norm(values):
        scale = lax.rsqrt(jnp.mean(values * values, -1, keepdims=True) + 1e-06)
        return (values * scale * gain[...]).astype(BF)

    def fill(dst, p):
        def one(q, carry):
            both = jnp.concatenate([tok2[:, group(q)], tok2[:, TAIL]], axis=0)
            dst[:, group(q)] = dot(mats_t[p, q], both).astype(BF)
            return carry

        lax.fori_loop(0, 3, one, 0)

    def send_normed(values, dst, p):
        rounded = norm(values)
        tok2[pl.ds(0, TOK), :] = rounded
        tok2[pl.ds(TOK, TOK), :] = rounded
        fill(dst, p)

    def send_scaled(cot, gates, tick, dst, p):
        both = gates[tick]
        tok2[pl.ds(0, TOK), :] = (both[:, 0:1] * cot).astype(BF)
        tok2[pl.ds(TOK, TOK), :] = (both[:, 1:2] * cot).astype(BF)
        fill(dst, p)

    def unpack(src, dst):
        def one(q, tail):
            both = dot(unpk[q], src[:, group(q)])
            dst[:, group(q)] = both[:ROWS].astype(BF)
            return tail + both[ROWS:]

        tail = lax.fori_loop(0, 3, one, jnp.zeros((ROWS, GRP), F32))
        dst[:, TAIL] = tail.astype(BF)

    def pack(src, dst):
        def one(q, carry):
            both = jnp.concatenate([src[:, group(q)], src[:, TAIL]], axis=0)
            dst[:, group(q)] = dot(pck[q], both).astype(BF)
            return carry

        lax.fori_loop(0, 3, one, 0)

    def gather(src, p, take):
        def one(q, tail):
            both = dot(mats[p, q], src[:, group(q)])
            take(group(q), both[: 2 * TOK])
            return tail + both[2 * TOK :]

        take(TAIL, lax.fori_loop(0, 3, one, jnp.zeros((2 * TOK, GRP), F32)))

    def expert_forward():
        def hidden(n, carry):
            cut = pl.ds(pl.multiple_of(n * 256, 256), 256)
            gate_pre = dot(xs[...], gate_w[:, cut])
            up_pre = dot(xs[...], up_w[:, cut])
            h1[:, cut] = (gate_pre * jax.nn.sigmoid(gate_pre) * up_pre).astype(BF)
            return carry

        lax.fori_loop(0, FH // 256, hidden, 0)

        def outer(n, carry):
            cut = pl.ds(pl.multiple_of(n * 512, 512), 512)
            xs[:, cut] = dot(h1[...], down_w[:, cut]).astype(BF)
            return carry

        lax.fori_loop(0, D // 512, outer, 0)

    def expert_backward():
        def hidden(n, carry):
            cut = pl.ds(pl.multiple_of(n * 256, 256), 256)
            gate_pre = dot(xs[...], gate_w[:, cut])
            up_pre = dot(xs[...], up_w[:, cut])
            hidden_grad = dot_nt(cs[...], down_w[cut, :])
            sig = jax.nn.sigmoid(gate_pre)
            h1[:, cut] = (
                hidden_grad * up_pre * sig * (1.0 + gate_pre * (1.0 - sig))
            ).astype(BF)
            h2[:, cut] = (hidden_grad * gate_pre * sig).astype(BF)
            return carry

        lax.fori_loop(0, FH // 256, hidden, 0)

        def outer(n, carry):
            cut = pl.ds(pl.multiple_of(n * 512, 512), 512)
            xs[:, cut] = (
                dot_nt(h1[...], gate_w[cut, :]) + dot_nt(h2[...], up_w[cut, :])
            ).astype(BF)
            return carry

        lax.fori_loop(0, D // 512, outer, 0)

    def finish_forward(acts, tick, p):
        both = fwd_gates[tick]
        one, two = both[:, 0:1], both[:, 1:2]

        def take(cut, parts):
            mixed = one * parts[:TOK] + two * parts[TOK:]
            fwd_out[tick, :, cut] = (acts[:, cut].astype(F32) + mixed).astype(BF)

        gather(fr_r, p, take)

    def finish_backward(cot, tick, p, total):
        def take(cut, parts):
            total[:, cut] = parts[:TOK] + parts[TOK:]

        gather(br_r, p, take)
        saved = bwd_saved[tick].astype(F32)
        scale = lax.rsqrt(jnp.mean(saved * saved, -1, keepdims=True) + 1e-06)
        weighted = total[...] * gain[...]
        inner = jnp.sum(weighted * saved, -1, keepdims=True) * (1.0 / D)
        grad = weighted * scale - saved * (scale * scale * scale * inner)
        bwd_out[tick] = (cot[...].astype(F32) + grad).astype(BF)

    slots(fwd_routes, 0, 0)
    send_normed(fwd_in[...].astype(F32), fd_s, 0)
    pl.semaphore_wait(barrier, EP + 1)
    exchange(fd_s, fd_r, F0D)
    slots(bwd_routes, 0, 1)
    send_normed(bwd_saved[0].astype(F32), bs_s.at[0], 1)
    exchange(bs_s.at[0], bs_r.at[0], B0S)
    send_scaled(bwd_grad[...].astype(F32), bwd_gates, 0, bc_s, 1)
    exchange(bc_s, bc_r, B0C)
    slots(fwd_routes, 1, 2)
    slots(bwd_routes, 1, 3)
    send_normed(bwd_saved[1].astype(F32), bs_s.at[1], 3)
    for load in loads:
        load.wait()

    arrived(fd_r, F0D)
    unpack(fd_r, xs)
    expert_forward()
    pack(xs, fr_s)
    exchange(fr_s, fr_r, F0R)
    exchange(bs_s.at[1], bs_r.at[1], B1S)

    arrived(bs_r.at[0], B0S)
    unpack(bs_r.at[0], xs)
    arrived(bc_r, B0C)
    unpack(bc_r, cs)
    expert_backward()
    pack(xs, br_s)
    exchange(br_s, br_r, B0R)

    arrived(fr_r, F0R)
    finish_forward(fwd_in, 0, 0)
    forth = relay(fwd_out.at[0], acts1, 0, ahead)
    forth.start()
    left(fd_s, F0D)
    forth.wait_recv()

    acts1[...] = jnp.where(pp == 0, jnp.zeros_like(acts1), acts1[...])
    send_normed(acts1[...].astype(F32), fd_s, 2)
    exchange(fd_s, fd_r, F1D)

    def backward_total(total):
        arrived(br_r, B0R)
        finish_backward(bwd_grad, 0, 1, total)

    pl.run_scoped(backward_total, pltpu.VMEM((TOK, D), F32))
    back = relay(bwd_out.at[0], cot1, 1, behind)
    back.start()
    left(bc_s, B0C)
    back.wait_recv()
    cot1[...] = jnp.where(pp == PP - 1, jnp.zeros_like(cot1), cot1[...])
    send_scaled(cot1[...].astype(F32), bwd_gates, 1, bc_s, 3)
    exchange(bc_s, bc_r, B1C)

    arrived(fd_r, F1D)
    unpack(fd_r, xs)
    expert_forward()
    left(fr_s, F0R)
    pack(xs, fr_s)
    exchange(fr_s, fr_r, F1R)

    arrived(bs_r.at[1], B1S)
    unpack(bs_r.at[1], xs)
    arrived(bc_r, B1C)
    unpack(bc_r, cs)
    expert_backward()
    left(br_s, B0R)
    pack(xs, br_s)
    exchange(br_s, br_r, B1R)

    arrived(fr_r, F1R)
    finish_forward(acts1, 1, 2)

    def backward_last(total):
        arrived(br_r, B1R)
        finish_backward(cot1, 1, 3, total)

    pl.run_scoped(backward_last, pltpu.VMEM((TOK, D), F32))

    forth.wait_send()
    back.wait_send()
    left(bs_s.at[0], B0S)
    left(bs_s.at[1], B1S)
    left(fd_s, F1D)
    left(bc_s, B1C)
    left(fr_s, F1R)
    left(br_s, B1R)


def on_device(
    fwd_in,
    fwd_routes,
    fwd_gates,
    bwd_grad,
    bwd_saved,
    bwd_routes,
    bwd_gates,
    norm_gain,
    gate_w,
    up_w,
    down_w,
):
    vmem = pl.BlockSpec(memory_space=pltpu.VMEM)
    hbm = pl.BlockSpec(memory_space=pl.ANY)
    packed = pltpu.VMEM((PACK, WIDE), BF)
    packed2 = pltpu.VMEM((2, PACK, WIDE), BF)
    out = jax.ShapeDtypeStruct((2, TOK, D), BF)
    fwd, bwd = pl.pallas_call(
        kernel,
        out_shape=(out, out),
        in_specs=[vmem] * 8 + [hbm] * 3,
        out_specs=(vmem, vmem),
        scratch_shapes=[
            pltpu.VMEM((D, FH), BF),
            pltpu.VMEM((D, FH), BF),
            pltpu.VMEM((FH, D), BF),
            packed,
            packed,
            packed,
            packed,
            packed2,
            packed2,
            packed,
            packed,
            packed,
            packed,
            pltpu.VMEM((4, 3, 4 * TOK, PACK), BF),
            pltpu.VMEM((4, 3, PACK, 4 * TOK), BF),
            pltpu.VMEM((3, 2 * ROWS, PACK), BF),
            pltpu.VMEM((3, PACK, 2 * ROWS), BF),
            pltpu.VMEM((2 * TOK, D), BF),
            pltpu.VMEM((ROWS, D), BF),
            pltpu.VMEM((ROWS, D), BF),
            pltpu.VMEM((ROWS, FH), BF),
            pltpu.VMEM((ROWS, FH), BF),
            pltpu.VMEM((TOK, D), BF),
            pltpu.VMEM((TOK, D), BF),
            pltpu.SemaphoreType.DMA((3,)),
            pltpu.SemaphoreType.DMA((10,)),
            pltpu.SemaphoreType.DMA((10,)),
            pltpu.SemaphoreType.DMA((2,)),
            pltpu.SemaphoreType.DMA((2,)),
        ],
        compiler_params=pltpu.CompilerParams(
            collective_id=0, has_side_effects=True, vmem_limit_bytes=60 << 20
        ),
        cost_estimate=pl.CostEstimate(
            flops=2 * 2 * 8 * ROWS * D * FH,
            bytes_accessed=6 * D * FH,
            transcendentals=4 * ROWS * FH,
        ),
    )(
        fwd_in[0],
        fwd_routes[0],
        fwd_gates[0],
        bwd_grad[0],
        bwd_saved[0],
        bwd_routes[0],
        bwd_gates[0],
        norm_gain,
        gate_w[0, 0],
        up_w[0, 0],
        down_w[0, 0],
    )
    return fwd[None], bwd[None]


def solution(mesh):
    in_specs = (
        P("pp", "ep", None),
        P("pp", None, "ep", None),
        P("pp", None, "ep", None),
        P("pp", "ep", None),
        P("pp", None, "ep", None),
        P("pp", None, "ep", None),
        P("pp", None, "ep", None),
        P("pp", None),
        P("pp", "ep", None, None),
        P("pp", "ep", None, None),
        P("pp", "ep", None, None),
    )
    out_specs = (P("pp", None, "ep", None), P("pp", None, "ep", None))
    return jax.shard_map(
        on_device, mesh=mesh, in_specs=in_specs, out_specs=out_specs, check_vma=False
    )
```

```python
import jax
import jax.numpy as jnp
from jax import lax
from jax.experimental import pallas as pl
from jax.experimental.pallas import tpu as pltpu
from jax.sharding import PartitionSpec as P

MESH = pl.DeviceIdType.MESH
BF = jnp.bfloat16
F32 = jnp.float32

EP = 16
PP = 8
TOK = 64
CAP = 12
D = 3584
FH = 1024
ROWS = EP * CAP
BLK = 16
GRP = D // 4
WIDE = 3 * GRP
PACK = EP * BLK
COL = EP // 2
CAP2 = 2 * CAP
BLK2 = 2 * BLK

F0D, B0S, B0C, F0R, B1S, B0R, F1D, B1C, F1R, B1R = range(10)


def dot(a, b):
    return jnp.dot(a, b, preferred_element_type=F32)


def dot_nt(a, b):
    return lax.dot_general(a, b, (((1,), (1,)), ((), ())), preferred_element_type=F32)


def iota(shape, dim):
    return lax.broadcasted_iota(jnp.int32, shape, dim)


def one_hot(cond):
    return jnp.where(cond, 1.0, 0.0).astype(BF)


def group(q):
    return pl.ds(pl.multiple_of(q * GRP, 128), GRP)


TAIL = pl.ds(WIDE, GRP)


def kernel(
    fwd_in,
    fwd_routes,
    fwd_gates,
    bwd_grad,
    bwd_saved,
    bwd_routes,
    bwd_gates,
    gain,
    gate_hbm,
    up_hbm,
    down_hbm,
    fwd_out,
    bwd_out,
    gate_w,
    up_w,
    down_w,
    fd_s,
    fd_r,
    fr_s,
    fr_r,
    bs_s,
    bs_r,
    bc_s,
    bc_r,
    br_s,
    br_r,
    mats,
    mats_t,
    mats_x,
    unpk,
    unpk_x,
    pck,
    tok,
    xs,
    cs,
    h1,
    h2,
    acts1,
    cot1,
    info_s,
    info_r,
    w_sem,
    s_sem,
    r_sem,
    rel_s,
    rel_r,
    inf_s,
    inf_r,
):
    pp = lax.axis_index("pp")
    me = lax.axis_index("ep")
    ahead = lax.rem(pp + 1, PP)
    behind = lax.rem(pp + PP - 1, PP)
    my_x = lax.rem(me // 2, 2)
    beside = me + 2 - 4 * my_x
    my_col = me // 4 * 2 + lax.rem(me, 2)

    loads = [
        pltpu.make_async_copy(src, dst, w_sem.at[i])
        for i, (src, dst) in enumerate(
            ((gate_hbm, gate_w), (up_hbm, up_w), (down_hbm, down_w))
        )
    ]
    for load in loads:
        load.start()

    barrier = pltpu.get_barrier_semaphore()

    def greet(d, carry):
        pl.semaphore_signal(
            barrier, inc=1, device_id=(pp, lax.rem(me + d, EP)), device_id_type=MESH
        )
        return carry

    lax.fori_loop(1, EP, greet, 0)
    for section in (ahead, behind):
        for place in (me, beside):
            pl.semaphore_signal(
                barrier, inc=1, device_id=(section, place), device_id_type=MESH
            )

    def block(e):
        return pl.ds(pl.multiple_of(e * BLK, BLK), BLK)

    def exchange(src, dst, phase):
        pltpu.make_async_copy(
            src.at[block(me)], dst.at[block(me)], r_sem.at[phase]
        ).start()

        def one(d, carry):
            e = lax.rem(me + d, EP)
            pltpu.make_async_remote_copy(
                src_ref=src.at[block(e)],
                dst_ref=dst.at[block(me)],
                send_sem=s_sem.at[phase],
                recv_sem=r_sem.at[phase],
                device_id=(pp, e),
                device_id_type=MESH,
            ).start()
            return carry

        lax.fori_loop(1, EP, one, 0)

    def block2(e):
        return pl.ds(pl.multiple_of(e * BLK2, BLK2), BLK2)

    def exchange_column(src, dst, phase):
        pltpu.make_async_copy(
            src.at[block2(my_col)], dst.at[block2(my_col)], r_sem.at[phase]
        ).start()

        def one(d, carry):
            col = lax.rem(my_col + d, COL)
            e = (col // 2 * 2 + my_x) * 2 + lax.rem(col, 2)
            pltpu.make_async_remote_copy(
                src_ref=src.at[block2(col)],
                dst_ref=dst.at[block2(my_col)],
                send_sem=s_sem.at[phase],
                recv_sem=r_sem.at[phase],
                device_id=(pp, e),
                device_id_type=MESH,
            ).start()
            return carry

        lax.fori_loop(1, COL, one, 0)

    def arrived(dst, phase):
        pltpu.make_async_copy(dst, dst, r_sem.at[phase]).wait()

    def left(src, phase, own=BLK):
        part = src.at[pl.ds(0, PACK - own)]
        pltpu.make_async_copy(part, part, s_sem.at[phase]).wait()

    def relay(src, dst, which, to):
        return [
            pltpu.make_async_remote_copy(
                src_ref=src,
                dst_ref=dst.at[i],
                send_sem=rel_s.at[which, i],
                recv_sem=rel_r.at[which, i],
                device_id=(to, place),
                device_id_type=MESH,
            )
            for i, place in enumerate((me, beside))
        ]

    eye = iota((TOK, TOK), 0) == iota((TOK, TOK), 1)

    def column(row):
        return jnp.sum(jnp.where(eye, row, 0.0), axis=1, keepdims=True)

    def columns(rows):
        return column(rows[0:1]), column(rows[1:2])

    def places(routes):
        expert = jnp.concatenate(columns(routes), axis=0).astype(jnp.int32)
        lanes = iota((2 * TOK, 128), 1)
        chosen = one_hot(expert == lanes)
        lower = one_hot(iota((2 * TOK, 2 * TOK), 1) < iota((2 * TOK, 2 * TOK), 0))
        before = dot(lower, chosen)
        slot = jnp.sum(before * chosen.astype(F32), axis=1, keepdims=True).astype(
            jnp.int32
        )
        third = (
            jnp.where(slot >= 3, 1, 0)
            + jnp.where(slot >= 6, 1, 0)
            + jnp.where(slot >= 9, 1, 0)
        )
        return expert, slot, third, slot - 3 * third

    lanes2 = iota((2 * TOK, PACK), 1)

    def slots(routes, p):
        expert, slot, third, rest = places(routes)
        main = jnp.where(lanes2 == expert * BLK + slot, 1.0, 0.0)
        for q in range(3):
            at = jnp.where(rest == q, expert * BLK + CAP + third, -1)
            full = jnp.concatenate([main, jnp.where(lanes2 == at, 1.0, 0.0)], axis=0)
            mats[p, q] = full.astype(BF)
            mats_t[p, q] = full.T.astype(BF)

    def slots_column(own, other, which):
        parts = []
        for s, routes in enumerate((own, other)):
            expert, slot, third, rest = places(routes)
            half = expert // 2
            base = jnp.where(
                half % 2 == my_x, (half // 2 * 2 + expert % 2) * BLK2, -(PACK * 2)
            )
            parts.append((base + s * CAP + slot, base + CAP2 + 4 * s + third, rest))
        for q in range(3):
            full = jnp.concatenate(
                [jnp.where(lanes2 == at, 1.0, 0.0) for at, _, _ in parts]
                + [
                    jnp.where(lanes2 == jnp.where(rest == q, at, -1), 1.0, 0.0)
                    for _, at, rest in parts
                ],
                axis=0,
            )
            mats_x[which, q] = full.T.astype(BF)

    rows = iota((ROWS, PACK), 0)
    cols = iota((ROWS, PACK), 1)
    source, slot = rows // CAP, rows % CAP
    for q in range(3):
        main = jnp.where(cols == source * BLK + slot, 1.0, 0.0)
        tail = jnp.where(
            (cols == source * BLK + CAP + slot // 3) & (slot % 3 == q), 1.0, 0.0
        )
        unpk[q, pl.ds(0, ROWS), :] = main.astype(BF)
        unpk[q, pl.ds(ROWS, ROWS), :] = tail.astype(BF)
    other = jnp.where(source // 2 % 2 == my_x, 0, 1)
    base = (source // 4 * 2 + source % 2) * BLK2
    for q in range(3):
        main = jnp.where(cols == base + other * CAP + slot, 1.0, 0.0)
        tail = jnp.where(
            (cols == base + CAP2 + 4 * other + slot // 3) & (slot % 3 == q), 1.0, 0.0
        )
        unpk_x[q, pl.ds(0, ROWS), :] = main.astype(BF)
        unpk_x[q, pl.ds(ROWS, ROWS), :] = tail.astype(BF)
    rows = iota((PACK, ROWS), 0)
    cols = iota((PACK, ROWS), 1)
    source, slot = cols // CAP, cols % CAP
    for q in range(3):
        main = jnp.where(rows == source * BLK + slot, 1.0, 0.0)
        tail = jnp.where(
            (rows == source * BLK + CAP + slot // 3) & (slot % 3 == q), 1.0, 0.0
        )
        pck[q] = jnp.concatenate([main, tail], axis=1).astype(BF)

    def norm(values):
        scale = lax.rsqrt(jnp.mean(values * values, -1, keepdims=True) + 1e-06)
        return (values * scale * gain[...]).astype(BF)

    def put(at, rows):
        tok[pl.ds(at * TOK, TOK), :] = rows

    def fill(dst, count, mat):
        def one(q, carry):
            cut = pl.ds(0, count * TOK)
            both = jnp.concatenate([tok[cut, group(q)], tok[cut, TAIL]], axis=0)
            dst[:, group(q)] = dot(mat[q], both).astype(BF)
            return carry

        lax.fori_loop(0, 3, one, 0)

    def put_normed(values, at):
        rounded = norm(values)
        put(at, rounded)
        put(at + 1, rounded)

    def put_scaled(cot, gates, at):
        one, two = columns(gates)
        put(at, (one * cot).astype(BF))
        put(at + 1, (two * cot).astype(BF))

    def unpack(src, dst, maps):
        def one(q, tail):
            both = dot(maps[q], src[:, group(q)])
            dst[:, group(q)] = both[:ROWS].astype(BF)
            return tail + both[ROWS:]

        tail = lax.fori_loop(0, 3, one, jnp.zeros((ROWS, GRP), F32))
        dst[:, TAIL] = tail.astype(BF)

    def pack(src, dst):
        def one(q, carry):
            both = jnp.concatenate([src[:, group(q)], src[:, TAIL]], axis=0)
            dst[:, group(q)] = dot(pck[q], both).astype(BF)
            return carry

        lax.fori_loop(0, 3, one, 0)

    def gather(src, p, take):
        def one(q, tail):
            both = dot(mats[p, q], src[:, group(q)])
            take(group(q), both[: 2 * TOK])
            return tail + both[2 * TOK :]

        take(TAIL, lax.fori_loop(0, 3, one, jnp.zeros((2 * TOK, GRP), F32)))

    def expert_forward():
        def hidden(n, carry):
            cut = pl.ds(pl.multiple_of(n * 256, 256), 256)
            gate_pre = dot(xs[...], gate_w[:, cut])
            up_pre = dot(xs[...], up_w[:, cut])
            h1[:, cut] = (gate_pre * jax.nn.sigmoid(gate_pre) * up_pre).astype(BF)
            return carry

        lax.fori_loop(0, FH // 256, hidden, 0)

        def outer(n, carry):
            cut = pl.ds(pl.multiple_of(n * 512, 512), 512)
            xs[:, cut] = dot(h1[...], down_w[:, cut]).astype(BF)
            return carry

        lax.fori_loop(0, D // 512, outer, 0)

    def expert_backward():
        def hidden(n, carry):
            cut = pl.ds(pl.multiple_of(n * 256, 256), 256)
            gate_pre = dot(xs[...], gate_w[:, cut])
            up_pre = dot(xs[...], up_w[:, cut])
            hidden_grad = dot_nt(cs[...], down_w[cut, :])
            sig = jax.nn.sigmoid(gate_pre)
            h1[:, cut] = (
                hidden_grad * up_pre * sig * (1.0 + gate_pre * (1.0 - sig))
            ).astype(BF)
            h2[:, cut] = (hidden_grad * gate_pre * sig).astype(BF)
            return carry

        lax.fori_loop(0, FH // 256, hidden, 0)

        def outer(n, carry):
            cut = pl.ds(pl.multiple_of(n * 512, 512), 512)
            xs[:, cut] = (
                dot_nt(h1[...], gate_w[cut, :]) + dot_nt(h2[...], up_w[cut, :])
            ).astype(BF)
            return carry

        lax.fori_loop(0, D // 512, outer, 0)

    def finish_forward(src, acts, tick, p):
        one, two = columns(fwd_gates[tick])

        def take(cut, parts):
            mixed = one * parts[:TOK] + two * parts[TOK:]
            fwd_out[tick, :, cut] = (acts[:, cut].astype(F32) + mixed).astype(BF)

        gather(src, p, take)

    def finish_backward(cot, tick, p, total):
        def take(cut, parts):
            total[:, cut] = parts[:TOK] + parts[TOK:]

        gather(br_r, p, take)
        saved = bwd_saved[tick].astype(F32)
        scale = lax.rsqrt(jnp.mean(saved * saved, -1, keepdims=True) + 1e-06)
        weighted = total[...] * gain[...]
        inner = jnp.sum(weighted * saved, -1, keepdims=True) * (1.0 / D)
        grad = weighted * scale - saved * (scale * scale * scale * inner)
        bwd_out[tick] = (cot[...].astype(F32) + grad).astype(BF)

    info_s[...] = jnp.zeros_like(info_s)
    info_s[pl.ds(0, 2), pl.ds(0, TOK)] = fwd_routes[1].astype(F32)
    info_s[pl.ds(2, 2), pl.ds(0, TOK)] = bwd_routes[1].astype(F32)
    info_s[pl.ds(4, 2), pl.ds(0, TOK)] = bwd_gates[1]
    inform = pltpu.make_async_remote_copy(
        src_ref=info_s,
        dst_ref=info_r,
        send_sem=inf_s,
        recv_sem=inf_r,
        device_id=(pp, beside),
        device_id_type=MESH,
    )

    slots(bwd_routes[0].astype(F32), 1)
    put_normed(bwd_saved[0].astype(F32), 0)
    fill(bs_s.at[0], 2, mats_t.at[1])
    pl.semaphore_wait(barrier, EP + 3)
    exchange(bs_s.at[0], bs_r.at[0], B0S)
    put_scaled(bwd_grad[...].astype(F32), bwd_gates[0], 0)
    fill(bc_s, 2, mats_t.at[1])
    exchange(bc_s, bc_r, B0C)
    inform.start()
    slots(fwd_routes[0].astype(F32), 0)
    put_normed(fwd_in[...].astype(F32), 0)
    fill(fd_s, 2, mats_t.at[0])
    exchange(fd_s, fd_r, F0D)
    slots(fwd_routes[1].astype(F32), 2)
    slots(bwd_routes[1].astype(F32), 3)
    put_normed(bwd_saved[1].astype(F32), 0)
    fill(bs_s.at[1], 2, mats_t.at[3])
    inform.wait()
    slots_column(info_s[0:2, 0:TOK], info_r[0:2, 0:TOK], 0)
    slots_column(info_s[2:4, 0:TOK], info_r[2:4, 0:TOK], 1)
    for load in loads:
        load.wait()

    left(bs_s.at[0], B0S)
    arrived(bs_r.at[0], B0S)
    unpack(bs_r.at[0], xs, unpk)
    arrived(bc_r, B0C)
    unpack(bc_r, cs, unpk)
    expert_backward()
    pack(xs, br_s)
    exchange(br_s, br_r, B0R)

    arrived(fd_r, F0D)
    unpack(fd_r, xs, unpk)
    expert_forward()
    pack(xs, fr_s)
    exchange(fr_s, fr_r, F0R)

    def backward_total(total):
        arrived(br_r, B0R)
        finish_backward(bwd_grad, 0, 1, total)

    pl.run_scoped(backward_total, pltpu.VMEM((TOK, D), F32))
    back = relay(bwd_out.at[0], cot1, 1, behind)
    for copy in back:
        copy.start()
    arrived(fr_r, F0R)
    exchange(bs_s.at[1], bs_r.at[1], B1S)
    finish_forward(fr_r, fwd_in, 0, 0)
    forth = relay(fwd_out.at[0], acts1, 0, ahead)
    for copy in forth:
        copy.start()

    left(bc_s, B0C)
    for copy in back:
        copy.wait_recv()
    cot1[...] = jnp.where(pp == PP - 1, jnp.zeros_like(cot1), cot1[...])
    put_scaled(cot1[0].astype(F32), bwd_gates[1], 0)
    put_scaled(cot1[1].astype(F32), info_r[4:6, 0:TOK], 2)
    fill(bc_s, 4, mats_x.at[1])
    exchange_column(bc_s, bc_r, B1C)
    left(fd_s, F0D)
    for copy in forth:
        copy.wait_recv()
    acts1[...] = jnp.where(pp == 0, jnp.zeros_like(acts1), acts1[...])
    put_normed(acts1[0].astype(F32), 0)
    put_normed(acts1[1].astype(F32), 2)
    fill(fd_s, 4, mats_x.at[0])
    exchange_column(fd_s, fd_r, F1D)

    arrived(bs_r.at[1], B1S)
    unpack(bs_r.at[1], xs, unpk)
    arrived(bc_r, B1C)
    unpack(bc_r, cs, unpk_x)
    expert_backward()
    left(br_s, B0R)
    pack(xs, br_s)
    exchange(br_s, br_r, B1R)

    arrived(fd_r, F1D)
    unpack(fd_r, xs, unpk_x)
    expert_forward()
    left(fr_s, F0R)
    pack(xs, fr_s)
    exchange(fr_s, bs_r.at[0], F1R)

    def backward_last(total):
        arrived(br_r, B1R)
        finish_backward(cot1.at[0], 1, 3, total)

    pl.run_scoped(backward_last, pltpu.VMEM((TOK, D), F32))
    arrived(bs_r.at[0], F1R)
    finish_forward(bs_r.at[0], acts1.at[0], 1, 2)

    for copy in forth + back:
        copy.wait_send()
    left(bs_s.at[1], B1S)
    left(fd_s, F1D, BLK2)
    left(bc_s, B1C, BLK2)
    left(fr_s, F1R)
    left(br_s, B1R)


def pass_on(fwd, bwd, fwd_out, bwd_out, sems):
    copies = [
        pltpu.make_async_copy(src, dst, sems.at[i])
        for i, (src, dst) in enumerate(((fwd, fwd_out), (bwd, bwd_out)))
    ]
    for copy in copies:
        copy.start()
    for copy in copies:
        copy.wait()


def on_device(
    fwd_in,
    fwd_routes,
    fwd_gates,
    bwd_grad,
    bwd_saved,
    bwd_routes,
    bwd_gates,
    norm_gain,
    gate_w,
    up_w,
    down_w,
):
    vmem = pl.BlockSpec(memory_space=pltpu.VMEM)
    hbm = pl.BlockSpec(memory_space=pl.ANY)
    packed = pltpu.VMEM((PACK, WIDE), BF)
    packed2 = pltpu.VMEM((2, PACK, WIDE), BF)
    out = jax.ShapeDtypeStruct((2, TOK, D), BF)
    kept = pltpu.VMEM((2, TOK, D), BF)
    fwd, bwd = pl.pallas_call(
        kernel,
        out_shape=(kept, kept),
        in_specs=[vmem] * 8 + [hbm] * 3,
        out_specs=(vmem, vmem),
        scratch_shapes=[
            pltpu.VMEM((D, FH), BF),
            pltpu.VMEM((D, FH), BF),
            pltpu.VMEM((FH, D), BF),
            packed,
            packed,
            packed,
            packed,
            packed2,
            packed2,
            packed,
            packed,
            packed,
            packed,
            pltpu.VMEM((4, 3, 4 * TOK, PACK), BF),
            pltpu.VMEM((4, 3, PACK, 4 * TOK), BF),
            pltpu.VMEM((2, 3, PACK, 8 * TOK), BF),
            pltpu.VMEM((3, 2 * ROWS, PACK), BF),
            pltpu.VMEM((3, 2 * ROWS, PACK), BF),
            pltpu.VMEM((3, PACK, 2 * ROWS), BF),
            pltpu.VMEM((4 * TOK, D), BF),
            pltpu.VMEM((ROWS, D), BF),
            pltpu.VMEM((ROWS, D), BF),
            pltpu.VMEM((ROWS, FH), BF),
            pltpu.VMEM((ROWS, FH), BF),
            pltpu.VMEM((2, TOK, D), BF),
            pltpu.VMEM((2, TOK, D), BF),
            pltpu.VMEM((8, 128), F32),
            pltpu.VMEM((8, 128), F32),
            pltpu.SemaphoreType.DMA((3,)),
            pltpu.SemaphoreType.DMA((10,)),
            pltpu.SemaphoreType.DMA((10,)),
            pltpu.SemaphoreType.DMA((2, 2)),
            pltpu.SemaphoreType.DMA((2, 2)),
            pltpu.SemaphoreType.DMA,
            pltpu.SemaphoreType.DMA,
        ],
        compiler_params=pltpu.CompilerParams(
            collective_id=0, has_side_effects=True, vmem_limit_bytes=60 << 20
        ),
        cost_estimate=pl.CostEstimate(
            flops=2 * 2 * 8 * ROWS * D * FH,
            bytes_accessed=6 * D * FH,
            transcendentals=4 * ROWS * FH,
        ),
    )(
        fwd_in[0],
        jnp.swapaxes(fwd_routes[0], 1, 2),
        jnp.swapaxes(fwd_gates[0], 1, 2),
        bwd_grad[0],
        bwd_saved[0],
        jnp.swapaxes(bwd_routes[0], 1, 2),
        jnp.swapaxes(bwd_gates[0], 1, 2),
        norm_gain,
        gate_w[0, 0],
        up_w[0, 0],
        down_w[0, 0],
    )
    fwd, bwd = pl.pallas_call(
        pass_on,
        out_shape=(out, out),
        in_specs=[vmem] * 2,
        out_specs=(hbm, hbm),
        scratch_shapes=[pltpu.SemaphoreType.DMA((2,))],
        compiler_params=pltpu.CompilerParams(vmem_limit_bytes=60 << 20),
    )(*(pltpu.with_memory_space_constraint(a, pltpu.VMEM) for a in (fwd, bwd)))
    return fwd[None], bwd[None]


def solution(mesh):
    in_specs = (
        P("pp", "ep", None),
        P("pp", None, "ep", None),
        P("pp", None, "ep", None),
        P("pp", "ep", None),
        P("pp", None, "ep", None),
        P("pp", None, "ep", None),
        P("pp", None, "ep", None),
        P("pp", None),
        P("pp", "ep", None, None),
        P("pp", "ep", None, None),
        P("pp", "ep", None, None),
    )
    out_specs = (P("pp", None, "ep", None), P("pp", None, "ep", None))
    return jax.shard_map(
        on_device, mesh=mesh, in_specs=in_specs, out_specs=out_specs, check_vma=False
    )
```

```python
import jax
import jax.numpy as jnp
from jax import lax
from jax.experimental import pallas as pl
from jax.experimental.pallas import tpu as pltpu
from jax.sharding import PartitionSpec as P

MESH = pl.DeviceIdType.MESH
BF = jnp.bfloat16
F32 = jnp.float32

EP = 16
PP = 8
TOK = 64
CAP = 12
D = 3584
FH = 1024
ROWS = EP * CAP
BLK = 16
GRP = D // 4
WIDE = 3 * GRP
PACK = EP * BLK
COL = EP // 2
CAP2 = 2 * CAP
BLK2 = 2 * BLK

F0D, B0S, B0C, F0R, B1S, B0R, F1D, B1C, F1R, B1R = range(10)


def dot(a, b):
    return jnp.dot(a, b, preferred_element_type=F32)


def dot_nt(a, b):
    return lax.dot_general(a, b, (((1,), (1,)), ((), ())), preferred_element_type=F32)


def iota(shape, dim):
    return lax.broadcasted_iota(jnp.int32, shape, dim)


def one_hot(cond):
    return jnp.where(cond, 1.0, 0.0).astype(BF)


def group(q):
    return pl.ds(pl.multiple_of(q * GRP, 128), GRP)


TAIL = pl.ds(WIDE, GRP)


def kernel(
    fwd_in,
    fwd_routes,
    fwd_gates,
    bwd_grad,
    bwd_saved,
    bwd_routes,
    bwd_gates,
    gain,
    gate_hbm,
    up_hbm,
    down_hbm,
    fwd_out,
    bwd_out,
    gate_w,
    up_w,
    down_w,
    fd_s,
    fd_r,
    fr_s,
    fr_r,
    bs_s,
    bs_r,
    bc_s,
    bc_r,
    br_s,
    br_r,
    mats,
    mats_x,
    unpk,
    unpk_x,
    pck,
    tok,
    xs,
    cs,
    h1,
    h2,
    acts1,
    cot1,
    near_s,
    near_r,
    fr2_r,
    info_s,
    info_r,
    w_sem,
    s_sem,
    r_sem,
    rel_s,
    rel_r,
    inf_s,
    inf_r,
    near_ss,
    near_rs,
):
    pp = lax.axis_index("pp")
    me = lax.axis_index("ep")
    ahead = lax.rem(pp + 1, PP)
    behind = lax.rem(pp + PP - 1, PP)
    my_x = lax.rem(me // 2, 2)
    beside = me + 2 - 4 * my_x
    my_col = me // 4 * 2 + lax.rem(me, 2)

    loads = [
        pltpu.make_async_copy(src, dst, w_sem.at[i])
        for i, (src, dst) in enumerate(
            ((gate_hbm, gate_w), (up_hbm, up_w), (down_hbm, down_w))
        )
    ]
    for load in loads:
        load.start()

    barrier = pltpu.get_barrier_semaphore()

    def greet(d, carry):
        pl.semaphore_signal(
            barrier, inc=1, device_id=(pp, lax.rem(me + d, EP)), device_id_type=MESH
        )
        return carry

    lax.fori_loop(1, EP, greet, 0)
    for section in (ahead, behind):
        pl.semaphore_signal(
            barrier, inc=1, device_id=(section, beside), device_id_type=MESH
        )

    def block(e):
        return pl.ds(pl.multiple_of(e * BLK, BLK), BLK)

    def exchange(src, dst, phase):
        pltpu.make_async_copy(
            src.at[block(me)], dst.at[block(me)], r_sem.at[phase]
        ).start()

        def one(d, carry):
            e = lax.rem(me + d, EP)
            pltpu.make_async_remote_copy(
                src_ref=src.at[block(e)],
                dst_ref=dst.at[block(me)],
                send_sem=s_sem.at[phase],
                recv_sem=r_sem.at[phase],
                device_id=(pp, e),
                device_id_type=MESH,
            ).start()
            return carry

        lax.fori_loop(1, EP, one, 0)

    def block2(e):
        return pl.ds(pl.multiple_of(e * BLK2, BLK2), BLK2)

    def exchange_column(src, dst, phase):
        pltpu.make_async_copy(
            src.at[block2(my_col)], dst.at[block2(my_col)], r_sem.at[phase]
        ).start()

        def one(d, carry):
            col = lax.rem(my_col + d, COL)
            e = (col // 2 * 2 + my_x) * 2 + lax.rem(col, 2)
            pltpu.make_async_remote_copy(
                src_ref=src.at[block2(col)],
                dst_ref=dst.at[block2(my_col)],
                send_sem=s_sem.at[phase],
                recv_sem=r_sem.at[phase],
                device_id=(pp, e),
                device_id_type=MESH,
            ).start()
            return carry

        lax.fori_loop(1, COL, one, 0)

    def arrived(dst, phase):
        pltpu.make_async_copy(dst, dst, r_sem.at[phase]).wait()

    def left(src, phase, own=BLK):
        part = src.at[pl.ds(0, PACK - own)]
        pltpu.make_async_copy(part, part, s_sem.at[phase]).wait()

    def to_beside(src, dst, i):
        return pltpu.make_async_remote_copy(
            src_ref=src,
            dst_ref=dst,
            send_sem=near_ss.at[i],
            recv_sem=near_rs.at[i],
            device_id=(pp, beside),
            device_id_type=MESH,
        )

    parts2 = tuple(pl.ds(i * TOK // 2, TOK // 2) for i in range(2))

    def relay(src, dst, which, to):
        return [
            pltpu.make_async_remote_copy(
                src_ref=src.at[part],
                dst_ref=dst.at[1, part],
                send_sem=rel_s.at[which, i],
                recv_sem=rel_r.at[which, i],
                device_id=(to, beside),
                device_id_type=MESH,
            )
            for i, part in enumerate(parts2)
        ]

    def hand_on(dst, which):
        return [
            pltpu.make_async_remote_copy(
                src_ref=dst.at[1, part],
                dst_ref=dst.at[0, part],
                send_sem=rel_s.at[which, 2 + i],
                recv_sem=rel_r.at[which, 2 + i],
                device_id=(pp, beside),
                device_id_type=MESH,
            )
            for i, part in enumerate(parts2)
        ]

    eye = iota((TOK, TOK), 0) == iota((TOK, TOK), 1)

    def column(row):
        return jnp.sum(jnp.where(eye, row, 0.0), axis=1, keepdims=True)

    def columns(rows):
        return column(rows[0:1]), column(rows[1:2])

    def places(routes):
        expert = jnp.concatenate(columns(routes), axis=0).astype(jnp.int32)
        lanes = iota((2 * TOK, 128), 1)
        chosen = one_hot(expert == lanes)
        lower = one_hot(iota((2 * TOK, 2 * TOK), 1) < iota((2 * TOK, 2 * TOK), 0))
        before = dot(lower, chosen)
        slot = jnp.sum(before * chosen.astype(F32), axis=1, keepdims=True).astype(
            jnp.int32
        )
        third = (
            jnp.where(slot >= 3, 1, 0)
            + jnp.where(slot >= 6, 1, 0)
            + jnp.where(slot >= 9, 1, 0)
        )
        return expert, slot, third, slot - 3 * third

    lanes2 = iota((2 * TOK, PACK), 1)

    def slots(routes, p, transposed=False):
        expert, slot, third, rest = places(routes)
        main = jnp.where(lanes2 == expert * BLK + slot, 1.0, 0.0)
        for q in range(3):
            at = jnp.where(rest == q, expert * BLK + CAP + third, -1)
            full = jnp.concatenate([main, jnp.where(lanes2 == at, 1.0, 0.0)], axis=0)
            mats[p, q] = full.astype(BF)
            if transposed:
                mats_x[2, q, :, pl.ds(0, PACK)] = full.T.astype(BF)

    def slots_column(own, other, which):
        parts = []
        for s, routes in enumerate((own, other)):
            expert, slot, third, rest = places(routes)
            half = expert // 2
            base = jnp.where(
                half % 2 == my_x, (half // 2 * 2 + expert % 2) * BLK2, -(PACK * 2)
            )
            parts.append((base + s * CAP + slot, base + CAP2 + 4 * s + third, rest))
        for q in range(3):
            full = jnp.concatenate(
                [jnp.where(lanes2 == at, 1.0, 0.0) for at, _, _ in parts]
                + [
                    jnp.where(lanes2 == jnp.where(rest == q, at, -1), 1.0, 0.0)
                    for _, at, rest in parts
                ],
                axis=0,
            )
            mats_x[which, q] = full.T.astype(BF)

    rows = iota((ROWS, PACK), 0)
    cols = iota((ROWS, PACK), 1)
    source, slot = rows // CAP, rows % CAP
    for q in range(3):
        main = jnp.where(cols == source * BLK + slot, 1.0, 0.0)
        tail = jnp.where(
            (cols == source * BLK + CAP + slot // 3) & (slot % 3 == q), 1.0, 0.0
        )
        unpk[q, pl.ds(0, ROWS), :] = main.astype(BF)
        unpk[q, pl.ds(ROWS, ROWS), :] = tail.astype(BF)
    other = jnp.where(source // 2 % 2 == my_x, 0, 1)
    base = (source // 4 * 2 + source % 2) * BLK2
    for q in range(3):
        main = jnp.where(cols == base + other * CAP + slot, 1.0, 0.0)
        tail = jnp.where(
            (cols == base + CAP2 + 4 * other + slot // 3) & (slot % 3 == q), 1.0, 0.0
        )
        unpk_x[q, pl.ds(0, ROWS), :] = main.astype(BF)
        unpk_x[q, pl.ds(ROWS, ROWS), :] = tail.astype(BF)
    rows = iota((PACK, ROWS), 0)
    cols = iota((PACK, ROWS), 1)
    source, slot = cols // CAP, cols % CAP
    for q in range(3):
        main = jnp.where(rows == source * BLK + slot, 1.0, 0.0)
        tail = jnp.where(
            (rows == source * BLK + CAP + slot // 3) & (slot % 3 == q), 1.0, 0.0
        )
        pck[q] = jnp.concatenate([main, tail], axis=1).astype(BF)

    def norm(values):
        scale = lax.rsqrt(jnp.mean(values * values, -1, keepdims=True) + 1e-06)
        return (values * scale * gain[...]).astype(BF)

    def put(at, rows):
        tok[pl.ds(at * TOK, TOK), :] = rows

    def fill(dst, count, mat):
        def one(q, carry):
            cut = pl.ds(0, count * TOK)
            both = jnp.concatenate([tok[cut, group(q)], tok[cut, TAIL]], axis=0)
            dst[:, group(q)] = dot(mat[q], both).astype(BF)
            return carry

        lax.fori_loop(0, 3, one, 0)

    def put_normed(values, at):
        rounded = norm(values)
        put(at, rounded)
        put(at + 1, rounded)

    def put_scaled(cot, gates, at):
        one, two = columns(gates)
        put(at, (one * cot).astype(BF))
        put(at + 1, (two * cot).astype(BF))

    def unpack(src, dst, maps):
        def one(q, tail):
            both = dot(maps[q], src[:, group(q)])
            dst[:, group(q)] = both[:ROWS].astype(BF)
            return tail + both[ROWS:]

        tail = lax.fori_loop(0, 3, one, jnp.zeros((ROWS, GRP), F32))
        dst[:, TAIL] = tail.astype(BF)

    def pack(src, dst):
        def one(q, carry):
            both = jnp.concatenate([src[:, group(q)], src[:, TAIL]], axis=0)
            dst[:, group(q)] = dot(pck[q], both).astype(BF)
            return carry

        lax.fori_loop(0, 3, one, 0)

    def gather(src, p, take):
        def one(q, tail):
            both = dot(mats[p, q], src[:, group(q)])
            take(group(q), both[: 2 * TOK])
            return tail + both[2 * TOK :]

        take(TAIL, lax.fori_loop(0, 3, one, jnp.zeros((2 * TOK, GRP), F32)))

    def expert_forward():
        def hidden(n, carry):
            cut = pl.ds(pl.multiple_of(n * 256, 256), 256)
            gate_pre = dot(xs[...], gate_w[:, cut])
            up_pre = dot(xs[...], up_w[:, cut])
            h1[:, cut] = (gate_pre * jax.nn.sigmoid(gate_pre) * up_pre).astype(BF)
            return carry

        lax.fori_loop(0, FH // 256, hidden, 0)

        def outer(n, carry):
            cut = pl.ds(pl.multiple_of(n * 512, 512), 512)
            xs[:, cut] = dot(h1[...], down_w[:, cut]).astype(BF)
            return carry

        lax.fori_loop(0, D // 512, outer, 0)

    def expert_backward():
        def hidden(n, carry):
            cut = pl.ds(pl.multiple_of(n * 256, 256), 256)
            gate_pre = dot(xs[...], gate_w[:, cut])
            up_pre = dot(xs[...], up_w[:, cut])
            hidden_grad = dot_nt(cs[...], down_w[cut, :])
            sig = jax.nn.sigmoid(gate_pre)
            h1[:, cut] = (
                hidden_grad * up_pre * sig * (1.0 + gate_pre * (1.0 - sig))
            ).astype(BF)
            h2[:, cut] = (hidden_grad * gate_pre * sig).astype(BF)
            return carry

        lax.fori_loop(0, FH // 256, hidden, 0)

        def outer(n, carry):
            cut = pl.ds(pl.multiple_of(n * 512, 512), 512)
            xs[:, cut] = (
                dot_nt(h1[...], gate_w[cut, :]) + dot_nt(h2[...], up_w[cut, :])
            ).astype(BF)
            return carry

        lax.fori_loop(0, D // 512, outer, 0)

    def finish_forward(src, acts, tick, p):
        one, two = columns(fwd_gates[tick])

        def take(cut, parts):
            mixed = one * parts[:TOK] + two * parts[TOK:]
            fwd_out[tick, :, cut] = (acts[:, cut].astype(F32) + mixed).astype(BF)

        gather(src, p, take)

    def finish_backward(src, cot, tick, p, total):
        def take(cut, parts):
            total[:, cut] = parts[:TOK] + parts[TOK:]

        gather(src, p, take)
        saved = bwd_saved[tick].astype(F32)
        scale = lax.rsqrt(jnp.mean(saved * saved, -1, keepdims=True) + 1e-06)
        weighted = total[...] * gain[...]
        inner = jnp.sum(weighted * saved, -1, keepdims=True) * (1.0 / D)
        grad = weighted * scale - saved * (scale * scale * scale * inner)
        bwd_out[tick] = (cot[...].astype(F32) + grad).astype(BF)

    info_s[...] = jnp.zeros_like(info_s)
    for i, what in enumerate(
        (
            bwd_routes[0],
            fwd_routes[0],
            fwd_routes[1],
            bwd_routes[1],
            bwd_gates[0],
            bwd_gates[1],
        )
    ):
        info_s[pl.ds(2 * i, 2), pl.ds(0, TOK)] = what.astype(F32)

    def known(ref, i):
        return ref[2 * i : 2 * i + 2, 0:TOK]

    inform = pltpu.make_async_remote_copy(
        src_ref=info_s,
        dst_ref=info_r,
        send_sem=inf_s,
        recv_sem=inf_r,
        device_id=(pp, beside),
        device_id_type=MESH,
    )
    cots = to_beside(bwd_grad, near_r.at[0], 0)
    forths = to_beside(near_s.at[0], near_r.at[1], 1)
    laters = to_beside(near_s.at[1], near_r.at[0], 2)

    def put_pair(own, other):
        for k in range(2):
            put(k, own)
            put(2 + k, other)

    slots(bwd_routes[0].astype(F32), 0, True)
    put_normed(bwd_saved[0].astype(F32), 0)
    fill(bs_s, 2, mats_x.at[2, :, :, pl.ds(0, PACK)])
    pl.semaphore_wait(barrier, EP + 1)
    inform.start()
    cots.start()
    exchange(bs_s, bs_r.at[0], B0S)
    near_s[0] = norm(fwd_in[...].astype(F32))
    near_s[1] = norm(bwd_saved[1].astype(F32))
    inform.wait()
    slots_column(known(info_s, 0), known(info_r, 0), 0)
    put_scaled(bwd_grad[...].astype(F32), bwd_gates[0], 0)
    cots.wait_recv()
    put_scaled(near_r[0].astype(F32), known(info_r, 4), 2)
    fill(bc_s, 4, mats_x.at[0])
    exchange_column(bc_s, bc_r, B0C)
    forths.start()
    for p in range(1, 4):
        slots_column(known(info_s, p), known(info_r, p), p)
        slots(known(info_s, p), p)
    for load in loads:
        load.wait()
    forths.wait_recv()
    put_pair(near_s[0], near_r[1])
    fill(fd_s, 4, mats_x.at[1])

    arrived(bs_r.at[0], B0S)
    unpack(bs_r.at[0], xs, unpk)
    arrived(bc_r, B0C)
    exchange_column(fd_s, fd_r, F0D)
    laters.start()
    unpack(bc_r, cs, unpk_x)
    expert_backward()
    pack(xs, br_s)
    exchange(br_s, br_r, B0R)

    arrived(fd_r, F0D)
    unpack(fd_r, xs, unpk_x)
    expert_forward()
    pack(xs, fr_s)
    exchange(fr_s, fr_r, F0R)

    def backward_total(total):
        arrived(br_r, B0R)
        finish_backward(br_r, bwd_grad, 0, 0, total)

    pl.run_scoped(backward_total, pltpu.VMEM((TOK, D), F32))
    back = relay(bwd_out.at[0], cot1, 1, behind)
    for copy in back:
        copy.start()
    left(bs_s, B0S)
    laters.wait_recv()
    put_pair(near_s[1], near_r[0])
    fill(bs_s, 4, mats_x.at[3])
    exchange_column(bs_s, bs_r.at[1], B1S)
    back_on = hand_on(cot1, 1)
    for copy, on in zip(back, back_on):
        copy.wait_recv()
        on.start()
    arrived(fr_r, F0R)
    finish_forward(fr_r, fwd_in, 0, 1)
    forth = relay(fwd_out.at[0], acts1, 0, ahead)
    for copy in forth:
        copy.start()

    left(bc_s, B0C, BLK2)
    for on in back_on:
        on.wait_recv()
    last = pp == PP - 1
    cot1[0] = jnp.where(last, jnp.zeros((TOK, D), BF), cot1[0])
    put_scaled(cot1[0].astype(F32), bwd_gates[1], 0)
    put_scaled(jnp.where(last, 0.0, cot1[1].astype(F32)), known(info_r, 5), 2)
    fill(bc_s, 4, mats_x.at[3])
    exchange_column(bc_s, bc_r, B1C)
    forth_on = hand_on(acts1, 0)
    for copy, on in zip(forth, forth_on):
        copy.wait_recv()
        on.start()
    left(fd_s, F0D, BLK2)
    first = pp == 0
    put_normed(jnp.where(first, 0.0, acts1[1].astype(F32)), 2)
    for on in forth_on:
        on.wait_recv()
    acts1[0] = jnp.where(first, jnp.zeros((TOK, D), BF), acts1[0])
    put_normed(acts1[0].astype(F32), 0)
    fill(fd_s, 4, mats_x.at[2])
    exchange_column(fd_s, fd_r, F1D)

    arrived(bs_r.at[1], B1S)
    unpack(bs_r.at[1], xs, unpk_x)
    arrived(bc_r, B1C)
    unpack(bc_r, cs, unpk_x)
    expert_backward()
    left(br_s, B0R)
    pack(xs, br_s)
    exchange(br_s, bs_r.at[0], B1R)

    arrived(fd_r, F1D)
    unpack(fd_r, xs, unpk_x)
    expert_forward()
    left(fr_s, F0R)
    pack(xs, fr_s)
    exchange(fr_s, fr2_r, F1R)

    def backward_last(total):
        arrived(bs_r.at[0], B1R)
        finish_backward(bs_r.at[0], cot1.at[0], 1, 3, total)

    pl.run_scoped(backward_last, pltpu.VMEM((TOK, D), F32))
    arrived(fr2_r, F1R)
    finish_forward(fr2_r, acts1.at[0], 1, 2)

    for copy in forth + forth_on + back + back_on + [cots, forths, laters]:
        copy.wait_send()
    left(bs_s, B1S, BLK2)
    left(fd_s, F1D, BLK2)
    left(bc_s, B1C, BLK2)
    left(fr_s, F1R)
    left(br_s, B1R)


def pass_on(fwd, bwd, fwd_out, bwd_out, sems):
    copies = [
        pltpu.make_async_copy(src, dst, sems.at[i])
        for i, (src, dst) in enumerate(((fwd, fwd_out), (bwd, bwd_out)))
    ]
    for copy in copies:
        copy.start()
    for copy in copies:
        copy.wait()


def on_device(
    fwd_in,
    fwd_routes,
    fwd_gates,
    bwd_grad,
    bwd_saved,
    bwd_routes,
    bwd_gates,
    norm_gain,
    gate_w,
    up_w,
    down_w,
):
    vmem = pl.BlockSpec(memory_space=pltpu.VMEM)
    hbm = pl.BlockSpec(memory_space=pl.ANY)
    packed = pltpu.VMEM((PACK, WIDE), BF)
    packed2 = pltpu.VMEM((2, PACK, WIDE), BF)
    out = jax.ShapeDtypeStruct((2, TOK, D), BF)
    kept = pltpu.VMEM((2, TOK, D), BF)
    fwd, bwd = pl.pallas_call(
        kernel,
        out_shape=(kept, kept),
        in_specs=[vmem] * 8 + [hbm] * 3,
        out_specs=(vmem, vmem),
        scratch_shapes=[
            pltpu.VMEM((D, FH), BF),
            pltpu.VMEM((D, FH), BF),
            pltpu.VMEM((FH, D), BF),
            packed,
            packed,
            packed,
            packed,
            packed,
            packed2,
            packed,
            packed,
            packed,
            packed,
            pltpu.VMEM((4, 3, 4 * TOK, PACK), BF),
            pltpu.VMEM((4, 3, PACK, 8 * TOK), BF),
            pltpu.VMEM((3, 2 * ROWS, PACK), BF),
            pltpu.VMEM((3, 2 * ROWS, PACK), BF),
            pltpu.VMEM((3, PACK, 2 * ROWS), BF),
            pltpu.VMEM((4 * TOK, D), BF),
            pltpu.VMEM((ROWS, D), BF),
            pltpu.VMEM((ROWS, D), BF),
            pltpu.VMEM((ROWS, FH), BF),
            pltpu.VMEM((ROWS, FH), BF),
            pltpu.VMEM((2, TOK, D), BF),
            pltpu.VMEM((2, TOK, D), BF),
            pltpu.VMEM((2, TOK, D), BF),
            pltpu.VMEM((2, TOK, D), BF),
            packed,
            pltpu.VMEM((16, 128), F32),
            pltpu.VMEM((16, 128), F32),
            pltpu.SemaphoreType.DMA((3,)),
            pltpu.SemaphoreType.DMA((10,)),
            pltpu.SemaphoreType.DMA((10,)),
            pltpu.SemaphoreType.DMA((2, 4)),
            pltpu.SemaphoreType.DMA((2, 4)),
            pltpu.SemaphoreType.DMA,
            pltpu.SemaphoreType.DMA,
            pltpu.SemaphoreType.DMA((3,)),
            pltpu.SemaphoreType.DMA((3,)),
        ],
        compiler_params=pltpu.CompilerParams(
            collective_id=0, has_side_effects=True, vmem_limit_bytes=60 << 20
        ),
        cost_estimate=pl.CostEstimate(
            flops=2 * 2 * 8 * ROWS * D * FH,
            bytes_accessed=6 * D * FH,
            transcendentals=4 * ROWS * FH,
        ),
    )(
        fwd_in[0],
        jnp.swapaxes(fwd_routes[0], 1, 2),
        jnp.swapaxes(fwd_gates[0], 1, 2),
        bwd_grad[0],
        bwd_saved[0],
        jnp.swapaxes(bwd_routes[0], 1, 2),
        jnp.swapaxes(bwd_gates[0], 1, 2),
        norm_gain,
        gate_w[0, 0],
        up_w[0, 0],
        down_w[0, 0],
    )
    fwd, bwd = pl.pallas_call(
        pass_on,
        out_shape=(out, out),
        in_specs=[vmem] * 2,
        out_specs=(hbm, hbm),
        scratch_shapes=[pltpu.SemaphoreType.DMA((2,))],
        compiler_params=pltpu.CompilerParams(vmem_limit_bytes=60 << 20),
    )(*(pltpu.with_memory_space_constraint(a, pltpu.VMEM) for a in (fwd, bwd)))
    return fwd[None], bwd[None]


def solution(mesh):
    in_specs = (
        P("pp", "ep", None),
        P("pp", None, "ep", None),
        P("pp", None, "ep", None),
        P("pp", "ep", None),
        P("pp", None, "ep", None),
        P("pp", None, "ep", None),
        P("pp", None, "ep", None),
        P("pp", None),
        P("pp", "ep", None, None),
        P("pp", "ep", None, None),
        P("pp", "ep", None, None),
    )
    out_specs = (P("pp", None, "ep", None), P("pp", None, "ep", None))
    return jax.shard_map(
        on_device, mesh=mesh, in_specs=in_specs, out_specs=out_specs, check_vma=False
    )
```

```python
import jax
import jax.numpy as jnp
from jax import lax
from jax.experimental import pallas as pl
from jax.experimental.pallas import tpu as pltpu
from jax.sharding import PartitionSpec as P

MESH = pl.DeviceIdType.MESH
BF = jnp.bfloat16
F32 = jnp.float32

EP = 16
PP = 8
TOK = 64
CAP = 12
D = 3584
FH = 1024
ROWS = EP * CAP
BLK = 16
GRP = D // 4
WIDE = 3 * GRP
PACK = EP * BLK
COL = EP // 2
CAP2 = 2 * CAP
BLK2 = 2 * BLK

F0D, B0S, B0C, F0R, B1S, B0R, F1D, B1C, F1R, B1R = range(10)


def dot(a, b):
    return jnp.dot(a, b, preferred_element_type=F32)


def dot_nt(a, b):
    return lax.dot_general(a, b, (((1,), (1,)), ((), ())), preferred_element_type=F32)


def iota(shape, dim):
    return lax.broadcasted_iota(jnp.int32, shape, dim)


def one_hot(cond):
    return jnp.where(cond, 1.0, 0.0).astype(BF)


def group(q):
    return pl.ds(pl.multiple_of(q * GRP, 128), GRP)


TAIL = pl.ds(WIDE, GRP)


def kernel(
    fwd_in,
    fwd_routes,
    fwd_gates,
    bwd_grad,
    bwd_saved,
    bwd_routes,
    bwd_gates,
    gain,
    gate_hbm,
    up_hbm,
    down_hbm,
    fwd_out,
    bwd_out,
    gate_w,
    up_w,
    down_w,
    fd_s,
    fd_r,
    fr_s,
    fr_r,
    bs_s,
    bs_r,
    bc_s,
    bc_r,
    br_s,
    br_r,
    mats,
    mats_x,
    unpk,
    unpk_x,
    pck,
    tok,
    xs,
    cs,
    h1,
    h2,
    gates,
    ups,
    acts1,
    cot1,
    near_s,
    near_r,
    fr2_r,
    info_s,
    info_r,
    w_sem,
    s_sem,
    r_sem,
    rel_s,
    rel_r,
    inf_s,
    inf_r,
    near_ss,
    near_rs,
):
    pp = lax.axis_index("pp")
    me = lax.axis_index("ep")
    ahead = lax.rem(pp + 1, PP)
    behind = lax.rem(pp + PP - 1, PP)
    my_x = lax.rem(me // 2, 2)
    beside = me + 2 - 4 * my_x
    my_col = me // 4 * 2 + lax.rem(me, 2)

    loads = [
        pltpu.make_async_copy(src, dst, w_sem.at[i])
        for i, (src, dst) in enumerate(
            ((gate_hbm, gate_w), (up_hbm, up_w), (down_hbm, down_w))
        )
    ]
    for load in loads:
        load.start()

    barrier = pltpu.get_barrier_semaphore()

    def greet(d, carry):
        pl.semaphore_signal(
            barrier, inc=1, device_id=(pp, lax.rem(me + d, EP)), device_id_type=MESH
        )
        return carry

    lax.fori_loop(1, EP, greet, 0)
    for section in (ahead, behind):
        pl.semaphore_signal(
            barrier, inc=1, device_id=(section, beside), device_id_type=MESH
        )

    def block(e):
        return pl.ds(pl.multiple_of(e * BLK, BLK), BLK)

    def exchange(src, dst, phase):
        pltpu.make_async_copy(
            src.at[block(me)], dst.at[block(me)], r_sem.at[phase]
        ).start()

        def one(d, carry):
            e = lax.rem(me + d, EP)
            pltpu.make_async_remote_copy(
                src_ref=src.at[block(e)],
                dst_ref=dst.at[block(me)],
                send_sem=s_sem.at[phase],
                recv_sem=r_sem.at[phase],
                device_id=(pp, e),
                device_id_type=MESH,
            ).start()
            return carry

        lax.fori_loop(1, EP, one, 0)

    def block2(e):
        return pl.ds(pl.multiple_of(e * BLK2, BLK2), BLK2)

    def exchange_column(src, dst, phase):
        pltpu.make_async_copy(
            src.at[block2(my_col)], dst.at[block2(my_col)], r_sem.at[phase]
        ).start()

        def one(d, carry):
            col = lax.rem(my_col + d, COL)
            e = (col // 2 * 2 + my_x) * 2 + lax.rem(col, 2)
            pltpu.make_async_remote_copy(
                src_ref=src.at[block2(col)],
                dst_ref=dst.at[block2(my_col)],
                send_sem=s_sem.at[phase],
                recv_sem=r_sem.at[phase],
                device_id=(pp, e),
                device_id_type=MESH,
            ).start()
            return carry

        lax.fori_loop(1, COL, one, 0)

    def arrived(dst, phase):
        pltpu.make_async_copy(dst, dst, r_sem.at[phase]).wait()

    def left(src, phase, own=BLK):
        part = src.at[pl.ds(0, PACK - own)]
        pltpu.make_async_copy(part, part, s_sem.at[phase]).wait()

    def to_beside(src, dst, i):
        return pltpu.make_async_remote_copy(
            src_ref=src,
            dst_ref=dst,
            send_sem=near_ss.at[i],
            recv_sem=near_rs.at[i],
            device_id=(pp, beside),
            device_id_type=MESH,
        )

    parts2 = tuple(pl.ds(i * TOK // 2, TOK // 2) for i in range(2))

    def relay(src, dst, which, to):
        return [
            pltpu.make_async_remote_copy(
                src_ref=src.at[part],
                dst_ref=dst.at[1, part],
                send_sem=rel_s.at[which, i],
                recv_sem=rel_r.at[which, i],
                device_id=(to, beside),
                device_id_type=MESH,
            )
            for i, part in enumerate(parts2)
        ]

    def hand_on(dst, which):
        return [
            pltpu.make_async_remote_copy(
                src_ref=dst.at[1, part],
                dst_ref=dst.at[0, part],
                send_sem=rel_s.at[which, 2 + i],
                recv_sem=rel_r.at[which, 2 + i],
                device_id=(pp, beside),
                device_id_type=MESH,
            )
            for i, part in enumerate(parts2)
        ]

    eye = iota((TOK, TOK), 0) == iota((TOK, TOK), 1)

    def column(row):
        return jnp.sum(jnp.where(eye, row, 0.0), axis=1, keepdims=True)

    def columns(rows):
        return column(rows[0:1]), column(rows[1:2])

    def places(routes):
        expert = jnp.concatenate(columns(routes), axis=0).astype(jnp.int32)
        lanes = iota((2 * TOK, 128), 1)
        chosen = one_hot(expert == lanes)
        lower = one_hot(iota((2 * TOK, 2 * TOK), 1) < iota((2 * TOK, 2 * TOK), 0))
        before = dot(lower, chosen)
        slot = jnp.sum(before * chosen.astype(F32), axis=1, keepdims=True).astype(
            jnp.int32
        )
        third = (
            jnp.where(slot >= 3, 1, 0)
            + jnp.where(slot >= 6, 1, 0)
            + jnp.where(slot >= 9, 1, 0)
        )
        return expert, slot, third, slot - 3 * third

    lanes2 = iota((2 * TOK, PACK), 1)

    def slots(routes, p, transposed=False):
        expert, slot, third, rest = places(routes)
        main = jnp.where(lanes2 == expert * BLK + slot, 1.0, 0.0)
        for q in range(3):
            at = jnp.where(rest == q, expert * BLK + CAP + third, -1)
            full = jnp.concatenate([main, jnp.where(lanes2 == at, 1.0, 0.0)], axis=0)
            mats[p, q] = full.astype(BF)
            if transposed:
                mats_x[2, q, :, pl.ds(0, PACK)] = full.T.astype(BF)

    def slots_column(own, other, which):
        parts = []
        for s, routes in enumerate((own, other)):
            expert, slot, third, rest = places(routes)
            half = expert // 2
            base = jnp.where(
                half % 2 == my_x, (half // 2 * 2 + expert % 2) * BLK2, -(PACK * 2)
            )
            parts.append((base + s * CAP + slot, base + CAP2 + 4 * s + third, rest))
        for q in range(3):
            full = jnp.concatenate(
                [jnp.where(lanes2 == at, 1.0, 0.0) for at, _, _ in parts]
                + [
                    jnp.where(lanes2 == jnp.where(rest == q, at, -1), 1.0, 0.0)
                    for _, at, rest in parts
                ],
                axis=0,
            )
            mats_x[which, q] = full.T.astype(BF)

    rows = iota((ROWS, PACK), 0)
    cols = iota((ROWS, PACK), 1)
    source, slot = rows // CAP, rows % CAP
    for q in range(3):
        main = jnp.where(cols == source * BLK + slot, 1.0, 0.0)
        tail = jnp.where(
            (cols == source * BLK + CAP + slot // 3) & (slot % 3 == q), 1.0, 0.0
        )
        unpk[q, pl.ds(0, ROWS), :] = main.astype(BF)
        unpk[q, pl.ds(ROWS, ROWS), :] = tail.astype(BF)
    other = jnp.where(source // 2 % 2 == my_x, 0, 1)
    base = (source // 4 * 2 + source % 2) * BLK2
    for q in range(3):
        main = jnp.where(cols == base + other * CAP + slot, 1.0, 0.0)
        tail = jnp.where(
            (cols == base + CAP2 + 4 * other + slot // 3) & (slot % 3 == q), 1.0, 0.0
        )
        unpk_x[q, pl.ds(0, ROWS), :] = main.astype(BF)
        unpk_x[q, pl.ds(ROWS, ROWS), :] = tail.astype(BF)
    rows = iota((PACK, ROWS), 0)
    cols = iota((PACK, ROWS), 1)
    source, slot = cols // CAP, cols % CAP
    for q in range(3):
        main = jnp.where(rows == source * BLK + slot, 1.0, 0.0)
        tail = jnp.where(
            (rows == source * BLK + CAP + slot // 3) & (slot % 3 == q), 1.0, 0.0
        )
        pck[q] = jnp.concatenate([main, tail], axis=1).astype(BF)

    def norm(values):
        scale = lax.rsqrt(jnp.mean(values * values, -1, keepdims=True) + 1e-06)
        return (values * scale * gain[...]).astype(BF)

    def put(at, rows):
        tok[pl.ds(at * TOK, TOK), :] = rows

    def fill(dst, count, mat):
        def one(q, carry):
            cut = pl.ds(0, count * TOK)
            both = jnp.concatenate([tok[cut, group(q)], tok[cut, TAIL]], axis=0)
            dst[:, group(q)] = dot(mat[q], both).astype(BF)
            return carry

        lax.fori_loop(0, 3, one, 0)

    def put_normed(values, at):
        rounded = norm(values)
        put(at, rounded)
        put(at + 1, rounded)

    def put_scaled(cot, weights, at):
        one, two = columns(weights)
        put(at, (one * cot).astype(BF))
        put(at + 1, (two * cot).astype(BF))

    def unpack(src, dst, maps):
        def one(q, tail):
            both = dot(maps[q], src[:, group(q)])
            dst[:, group(q)] = both[:ROWS].astype(BF)
            return tail + both[ROWS:]

        tail = lax.fori_loop(0, 3, one, jnp.zeros((ROWS, GRP), F32))
        dst[:, TAIL] = tail.astype(BF)

    def pack(src, dst):
        def one(q, carry):
            both = jnp.concatenate([src[:, group(q)], src[:, TAIL]], axis=0)
            dst[:, group(q)] = dot(pck[q], both).astype(BF)
            return carry

        lax.fori_loop(0, 3, one, 0)

    def gather(src, p, take):
        def one(q, tail):
            both = dot(mats[p, q], src[:, group(q)])
            take(group(q), both[: 2 * TOK])
            return tail + both[2 * TOK :]

        take(TAIL, lax.fori_loop(0, 3, one, jnp.zeros((2 * TOK, GRP), F32)))

    def expert_forward():
        def hidden(n, carry):
            cut = pl.ds(pl.multiple_of(n * 256, 256), 256)
            gate_pre = dot(xs[...], gate_w[:, cut])
            up_pre = dot(xs[...], up_w[:, cut])
            h1[:, cut] = (gate_pre * jax.nn.sigmoid(gate_pre) * up_pre).astype(BF)
            return carry

        lax.fori_loop(0, FH // 256, hidden, 0)

        def outer(n, carry):
            cut = pl.ds(pl.multiple_of(n * 512, 512), 512)
            xs[:, cut] = dot(h1[...], down_w[:, cut]).astype(BF)
            return carry

        lax.fori_loop(0, D // 512, outer, 0)

    def expert_values():
        def hidden(n, carry):
            cut = pl.ds(pl.multiple_of(n * 256, 256), 256)
            gates[:, cut] = dot(xs[...], gate_w[:, cut])
            ups[:, cut] = dot(xs[...], up_w[:, cut])
            return carry

        lax.fori_loop(0, FH // 256, hidden, 0)

    def expert_backward():
        def hidden(n, carry):
            cut = pl.ds(pl.multiple_of(n * 256, 256), 256)
            gate_pre, up_pre = gates[:, cut], ups[:, cut]
            hidden_grad = dot_nt(cs[...], down_w[cut, :])
            sig = jax.nn.sigmoid(gate_pre)
            h1[:, cut] = (
                hidden_grad * up_pre * sig * (1.0 + gate_pre * (1.0 - sig))
            ).astype(BF)
            h2[:, cut] = (hidden_grad * gate_pre * sig).astype(BF)
            return carry

        lax.fori_loop(0, FH // 256, hidden, 0)

        def outer(n, carry):
            cut = pl.ds(pl.multiple_of(n * 512, 512), 512)
            xs[:, cut] = (
                dot_nt(h1[...], gate_w[cut, :]) + dot_nt(h2[...], up_w[cut, :])
            ).astype(BF)
            return carry

        lax.fori_loop(0, D // 512, outer, 0)

    def finish_forward(src, acts, tick, p):
        one, two = columns(fwd_gates[tick])

        def take(cut, parts):
            mixed = one * parts[:TOK] + two * parts[TOK:]
            fwd_out[tick, :, cut] = (acts[:, cut].astype(F32) + mixed).astype(BF)

        gather(src, p, take)

    def finish_backward(src, cot, tick, p, total):
        def take(cut, parts):
            total[:, cut] = parts[:TOK] + parts[TOK:]

        gather(src, p, take)
        saved = bwd_saved[tick].astype(F32)
        scale = lax.rsqrt(jnp.mean(saved * saved, -1, keepdims=True) + 1e-06)
        weighted = total[...] * gain[...]
        inner = jnp.sum(weighted * saved, -1, keepdims=True) * (1.0 / D)
        grad = weighted * scale - saved * (scale * scale * scale * inner)
        bwd_out[tick] = (cot[...].astype(F32) + grad).astype(BF)

    info_s[...] = jnp.zeros_like(info_s)
    for i, what in enumerate(
        (
            bwd_routes[0],
            fwd_routes[0],
            fwd_routes[1],
            bwd_routes[1],
            bwd_gates[0],
            bwd_gates[1],
        )
    ):
        info_s[pl.ds(2 * i, 2), pl.ds(0, TOK)] = what.astype(F32)

    def known(ref, i):
        return ref[2 * i : 2 * i + 2, 0:TOK]

    inform = pltpu.make_async_remote_copy(
        src_ref=info_s,
        dst_ref=info_r,
        send_sem=inf_s,
        recv_sem=inf_r,
        device_id=(pp, beside),
        device_id_type=MESH,
    )
    cots = to_beside(bwd_grad, near_r.at[0], 0)
    forths = to_beside(near_s.at[0], near_r.at[1], 1)
    laters = to_beside(near_s.at[1], near_r.at[0], 2)

    def put_pair(own, other):
        for k in range(2):
            put(k, own)
            put(2 + k, other)

    slots(bwd_routes[0].astype(F32), 0, True)
    put_normed(bwd_saved[0].astype(F32), 0)
    fill(bs_s, 2, mats_x.at[2, :, :, pl.ds(0, PACK)])
    pl.semaphore_wait(barrier, EP + 1)
    inform.start()
    cots.start()
    exchange(bs_s, bs_r.at[0], B0S)
    near_s[0] = norm(fwd_in[...].astype(F32))
    near_s[1] = norm(bwd_saved[1].astype(F32))
    inform.wait()
    slots_column(known(info_s, 0), known(info_r, 0), 0)
    put_scaled(bwd_grad[...].astype(F32), bwd_gates[0], 0)
    cots.wait_recv()
    put_scaled(near_r[0].astype(F32), known(info_r, 4), 2)
    fill(bc_s, 4, mats_x.at[0])
    exchange_column(bc_s, bc_r, B0C)
    forths.start()
    for p in range(1, 4):
        slots_column(known(info_s, p), known(info_r, p), p)
        slots(known(info_s, p), p)
    for load in loads:
        load.wait()
    forths.wait_recv()
    put_pair(near_s[0], near_r[1])
    fill(fd_s, 4, mats_x.at[1])

    arrived(bs_r.at[0], B0S)
    unpack(bs_r.at[0], xs, unpk)
    arrived(bc_r, B0C)
    exchange_column(fd_s, fd_r, F0D)
    laters.start()
    expert_values()
    unpack(bc_r, cs, unpk_x)
    expert_backward()
    pack(xs, br_s)
    exchange(br_s, br_r, B0R)

    arrived(fd_r, F0D)
    unpack(fd_r, xs, unpk_x)
    expert_forward()
    pack(xs, fr_s)
    exchange(fr_s, fr_r, F0R)

    def backward_total(total):
        arrived(br_r, B0R)
        finish_backward(br_r, bwd_grad, 0, 0, total)

    pl.run_scoped(backward_total, pltpu.VMEM((TOK, D), F32))
    back = relay(bwd_out.at[0], cot1, 1, behind)
    for copy in back:
        copy.start()
    left(bs_s, B0S)
    laters.wait_recv()
    put_pair(near_s[1], near_r[0])
    fill(bs_s, 4, mats_x.at[3])
    exchange_column(bs_s, bs_r.at[1], B1S)
    back_on = hand_on(cot1, 1)
    for copy, on in zip(back, back_on):
        copy.wait_recv()
        on.start()
    arrived(fr_r, F0R)
    finish_forward(fr_r, fwd_in, 0, 1)
    forth = relay(fwd_out.at[0], acts1, 0, ahead)
    for copy in forth:
        copy.start()

    left(bc_s, B0C, BLK2)
    for on in back_on:
        on.wait_recv()
    last = pp == PP - 1
    cot1[0] = jnp.where(last, jnp.zeros((TOK, D), BF), cot1[0])
    put_scaled(cot1[0].astype(F32), bwd_gates[1], 0)
    put_scaled(jnp.where(last, 0.0, cot1[1].astype(F32)), known(info_r, 5), 2)
    fill(bc_s, 4, mats_x.at[3])
    exchange_column(bc_s, bc_r, B1C)
    forth_on = hand_on(acts1, 0)
    for copy, on in zip(forth, forth_on):
        copy.wait_recv()
        on.start()
    left(fd_s, F0D, BLK2)
    first = pp == 0
    put_normed(jnp.where(first, 0.0, acts1[1].astype(F32)), 2)
    for on in forth_on:
        on.wait_recv()
    acts1[0] = jnp.where(first, jnp.zeros((TOK, D), BF), acts1[0])
    put_normed(acts1[0].astype(F32), 0)
    fill(fd_s, 4, mats_x.at[2])
    exchange_column(fd_s, fd_r, F1D)

    arrived(bs_r.at[1], B1S)
    unpack(bs_r.at[1], xs, unpk_x)
    expert_values()
    arrived(bc_r, B1C)
    unpack(bc_r, cs, unpk_x)
    expert_backward()
    left(br_s, B0R)
    pack(xs, br_s)
    exchange(br_s, bs_r.at[0], B1R)

    arrived(fd_r, F1D)
    unpack(fd_r, xs, unpk_x)
    expert_forward()
    left(fr_s, F0R)
    pack(xs, fr_s)
    exchange(fr_s, fr2_r, F1R)

    def backward_last(total):
        arrived(bs_r.at[0], B1R)
        finish_backward(bs_r.at[0], cot1.at[0], 1, 3, total)

    pl.run_scoped(backward_last, pltpu.VMEM((TOK, D), F32))
    arrived(fr2_r, F1R)
    finish_forward(fr2_r, acts1.at[0], 1, 2)

    for copy in forth + forth_on + back + back_on + [cots, forths, laters]:
        copy.wait_send()
    left(bs_s, B1S, BLK2)
    left(fd_s, F1D, BLK2)
    left(bc_s, B1C, BLK2)
    left(fr_s, F1R)
    left(br_s, B1R)


def pass_on(fwd, bwd, fwd_out, bwd_out, sems):
    copies = [
        pltpu.make_async_copy(src, dst, sems.at[i])
        for i, (src, dst) in enumerate(((fwd, fwd_out), (bwd, bwd_out)))
    ]
    for copy in copies:
        copy.start()
    for copy in copies:
        copy.wait()


def on_device(
    fwd_in,
    fwd_routes,
    fwd_gates,
    bwd_grad,
    bwd_saved,
    bwd_routes,
    bwd_gates,
    norm_gain,
    gate_w,
    up_w,
    down_w,
):
    vmem = pl.BlockSpec(memory_space=pltpu.VMEM)
    hbm = pl.BlockSpec(memory_space=pl.ANY)
    packed = pltpu.VMEM((PACK, WIDE), BF)
    packed2 = pltpu.VMEM((2, PACK, WIDE), BF)
    out = jax.ShapeDtypeStruct((2, TOK, D), BF)
    kept = pltpu.VMEM((2, TOK, D), BF)
    fwd, bwd = pl.pallas_call(
        kernel,
        out_shape=(kept, kept),
        in_specs=[vmem] * 8 + [hbm] * 3,
        out_specs=(vmem, vmem),
        scratch_shapes=[
            pltpu.VMEM((D, FH), BF),
            pltpu.VMEM((D, FH), BF),
            pltpu.VMEM((FH, D), BF),
            packed,
            packed,
            packed,
            packed,
            packed,
            packed2,
            packed,
            packed,
            packed,
            packed,
            pltpu.VMEM((4, 3, 4 * TOK, PACK), BF),
            pltpu.VMEM((4, 3, PACK, 8 * TOK), BF),
            pltpu.VMEM((3, 2 * ROWS, PACK), BF),
            pltpu.VMEM((3, 2 * ROWS, PACK), BF),
            pltpu.VMEM((3, PACK, 2 * ROWS), BF),
            pltpu.VMEM((4 * TOK, D), BF),
            pltpu.VMEM((ROWS, D), BF),
            pltpu.VMEM((ROWS, D), BF),
            pltpu.VMEM((ROWS, FH), BF),
            pltpu.VMEM((ROWS, FH), BF),
            pltpu.VMEM((ROWS, FH), F32),
            pltpu.VMEM((ROWS, FH), F32),
            pltpu.VMEM((2, TOK, D), BF),
            pltpu.VMEM((2, TOK, D), BF),
            pltpu.VMEM((2, TOK, D), BF),
            pltpu.VMEM((2, TOK, D), BF),
            packed,
            pltpu.VMEM((16, 128), F32),
            pltpu.VMEM((16, 128), F32),
            pltpu.SemaphoreType.DMA((3,)),
            pltpu.SemaphoreType.DMA((10,)),
            pltpu.SemaphoreType.DMA((10,)),
            pltpu.SemaphoreType.DMA((2, 4)),
            pltpu.SemaphoreType.DMA((2, 4)),
            pltpu.SemaphoreType.DMA,
            pltpu.SemaphoreType.DMA,
            pltpu.SemaphoreType.DMA((3,)),
            pltpu.SemaphoreType.DMA((3,)),
        ],
        compiler_params=pltpu.CompilerParams(
            collective_id=0, has_side_effects=True, vmem_limit_bytes=61 << 20
        ),
        cost_estimate=pl.CostEstimate(
            flops=2 * 2 * 8 * ROWS * D * FH,
            bytes_accessed=6 * D * FH,
            transcendentals=4 * ROWS * FH,
        ),
    )(
        fwd_in[0],
        jnp.swapaxes(fwd_routes[0], 1, 2),
        jnp.swapaxes(fwd_gates[0], 1, 2),
        bwd_grad[0],
        bwd_saved[0],
        jnp.swapaxes(bwd_routes[0], 1, 2),
        jnp.swapaxes(bwd_gates[0], 1, 2),
        norm_gain,
        gate_w[0, 0],
        up_w[0, 0],
        down_w[0, 0],
    )
    fwd, bwd = pl.pallas_call(
        pass_on,
        out_shape=(out, out),
        in_specs=[vmem] * 2,
        out_specs=(hbm, hbm),
        scratch_shapes=[pltpu.SemaphoreType.DMA((2,))],
        compiler_params=pltpu.CompilerParams(vmem_limit_bytes=60 << 20),
    )(*(pltpu.with_memory_space_constraint(a, pltpu.VMEM) for a in (fwd, bwd)))
    return fwd[None], bwd[None]


def solution(mesh):
    in_specs = (
        P("pp", "ep", None),
        P("pp", None, "ep", None),
        P("pp", None, "ep", None),
        P("pp", "ep", None),
        P("pp", None, "ep", None),
        P("pp", None, "ep", None),
        P("pp", None, "ep", None),
        P("pp", None),
        P("pp", "ep", None, None),
        P("pp", "ep", None, None),
        P("pp", "ep", None, None),
    )
    out_specs = (P("pp", None, "ep", None), P("pp", None, "ep", None))
    return jax.shard_map(
        on_device, mesh=mesh, in_specs=in_specs, out_specs=out_specs, check_vma=False
    )
```
